32 devices in a mesh: freq: 4 (over z), src: 8 (over y, x, core).
Axes of the slice: x: 2, y: 2, z: 4, core: 2. Of those that a mesh axis runs over, the one named last changes fastest.
Arguments:
- data: bfloat16 [2, 4, 128, 24576], P(None, 'freq', None, 'src'), may hold values from -6 to 6
- recip: bfloat16 [2, 4, 128, 128], P(None, 'freq', None, 'src'), may hold values from -6 to 6
- gap: int32 [128, 128], P(None, 'src'), may hold values 0 or 1
- owner: int32 [8], replicated, may hold values from 0 to 7, as said below
- weights: bfloat16 [2, 4, 24576, 64], P(None, 'freq', 'src'), may hold values from -0.0390625 to 0.0390625
- start_row: int32 [4], P('freq'), may hold values from 0 to 96, as said below
- end_row: int32 [4], P('freq'), may hold values from 32 to 128, as said below
- recorded: bfloat16 [192, 64, 128], P('freq', 'src'), may hold values from -6 to 6
Outputs:
- primaries: bfloat16 [192, 64, 128], P('freq', 'src')
- filters: float32 [4, 27], P('freq')
The draws below stay inside these ranges and needn't reach their ends.
Inputs may be any that keep to these rules, and one draw needn't show every extreme that they name: `owner`: a permutation: each block is named by exactly one src index. `start_row`: start of window i lies between i * 32 - 8 and i * 32, never before 0; window 1 starts exactly 8 early. `end_row`: end of window i lies between (i + 1) * 32 and (i + 1) * 32 + 8, never after 128; window 1 ends exactly 8 late.
All inputs are finite; a program needn't handle non-finite values. No bound on the sum of `gap` on one device may be relied on, other than what follows from the above.
Results may differ from the reference program's by a relative error of at most 0.001.
Values may be sent and summed in bfloat16 or wider, within the bound.
A program may use at most 64 MiB of HBM per device.

```python
import math
import jax
import jax.numpy as jnp
from jax import lax

RECV = 128
NFFT = 512
F_LOW = 40
K_DEV = 3072
T_DEV = 32
NEAR = 16
HALO = 8
LAGS_T = 9
LAGS_X = 3
NF = 4
KTOT = 24576
SOUT = 64
NT = 128
WROWS = 48
NU = 27
N_FREQ = 4
N_SRC = 8


def window_bounds(key):
    early = jax.random.randint(jax.random.fold_in(key, 11), (N_FREQ,), 0, HALO + 1)
    late = jax.random.randint(jax.random.fold_in(key, 12), (N_FREQ,), 0, HALO + 1)
    index = jnp.arange(N_FREQ, dtype=jnp.int32)
    early = jnp.where(index == 1, HALO, early)
    late = jnp.where(index == 1, HALO, late)
    first = jnp.maximum(index * T_DEV - early, 0)
    last = jnp.minimum((index + 1) * T_DEV + late, T_DEV * N_FREQ)
    return (first.astype(jnp.int32), last.astype(jnp.int32))


def draw_start_row(key, part):
    first, last = window_bounds(key)
    return first


def draw_end_row(key, part):
    first, last = window_bounds(key)
    return last


def draw_owner(key, part):
    key = jax.random.fold_in(key, 21)
    anchor = jax.random.randint(jax.random.fold_in(key, 1), (), 0, N_SRC).astype(jnp.int32)
    ranks = jax.random.permutation(jax.random.fold_in(key, 2), N_SRC).astype(jnp.int32) + 3
    index = jnp.arange(N_SRC, dtype=jnp.int32)
    second = (anchor + 1) % N_SRC
    third = (anchor + 1 + N_SRC // 2) % N_SRC
    ranks = jnp.where(index == anchor, 0, ranks)
    ranks = jnp.where(index == second, 1, ranks)
    ranks = jnp.where(index == third, 2, ranks)
    order = jnp.argsort(ranks, stable=True).astype(jnp.int32)
    after = jnp.roll(order, -1)
    return jnp.zeros((N_SRC,), jnp.int32).at[order].set(after)


def place_ends(result, stream_key, least, high):
    index_at = [jax.random.randint(jax.random.fold_in(stream_key, axis), (), 0, length) for axis, length in enumerate(result.shape)]
    main_axis = result.shape.index(max(result.shape))
    neighbour = index_at[:main_axis] + [(index_at[main_axis] + 1) % result.shape[main_axis]] + index_at[main_axis + 1:]
    return result.at[tuple(index_at)].set(least).at[tuple(neighbour)].set(high)


def raised(array, rng, source, target, blocks, factor):
    def block_of(axis_at):
        return (jnp.arange(array.shape[axis_at]) // (array.shape[axis_at] // blocks)).reshape((-1,) + (1,) * (array.ndim - 1 - axis_at))

    first = jax.random.permutation(rng, blocks)[block_of(target)]
    second = (block_of(target) + blocks // 2) % blocks
    return jnp.where((block_of(source) == first) | (block_of(source) == second), factor * array, array)


def block_scale(key, extent, split, smallest, high):
    loudness, own = 1.0, jax.random.fold_in(key, 6)
    for axis_at, parts in split:
        draws = jnp.exp(jax.random.uniform(jax.random.fold_in(own, axis_at), (parts,), jnp.float32, smallest / len(split), high / len(split)))
        loudness = loudness * jnp.repeat(draws, extent[axis_at] // parts).reshape([-1 if axis == axis_at else 1 for axis in range(len(extent))])
    return loudness


def centred(rng, dims, spread, limit, cuts=(), kind=jnp.bfloat16):
    values = spread * jax.random.normal(rng, dims, jnp.float32)
    if cuts:
        values = values * block_scale(rng, dims, cuts, -0.22, 0.18)
    return jnp.clip(values, -limit, limit).astype(kind)


def noise_with(stream_key, extent, spread, reach, cuts, heavy, held_as=jnp.bfloat16):
    result = spread * jax.random.normal(stream_key, extent, jnp.float32)
    if cuts:
        result = result * block_scale(stream_key, extent, cuts, -0.22, 0.18)
    return jnp.clip(raised(result, jax.random.fold_in(stream_key, 3), *heavy), -reach, reach).astype(held_as)


def setup_inputs(seed: int = 0) -> dict:
    seeds = jax.random.split(jax.random.key(seed), 9)
    return {
        "data": centred(seeds[0], (2, NF, RECV, KTOT), 1.0, 6.0, ((1, 4), (3, 8))),
        "recip": centred(seeds[1], (2, NF, RECV, NEAR * N_SRC), 1.0, 6.0, ((1, 4), (3, 8))),
        "gap": place_ends((jax.random.randint(seeds[2], (RECV, NEAR * N_SRC), 0, 2) < 1).astype(jnp.int32), jax.random.fold_in(seeds[2], 1), 0, 1),
        "owner": draw_owner(jax.random.fold_in(seeds[8], 71), 0),
        "weights": noise_with(seeds[4], (2, NF, KTOT, SOUT), (2 * KTOT) ** -0.5, 0.0390625, ((1, 4), (2, 8)), (2, 3, 8, 2.0)),
        "start_row": draw_start_row(jax.random.fold_in(seeds[8], 71), 0),
        "end_row": draw_end_row(jax.random.fold_in(seeds[8], 71), 0),
        "recorded": centred(seeds[7], (N_FREQ * WROWS, SOUT, RECV), 1.0, 6.0, ((0, 4), (1, 8))),
    }


def phase_tables(times, freqs):
    turns = (F_LOW + freqs)[None, :] * times[:, None] % NFFT
    angle = turns.astype(jnp.float32) * (2.0 * math.pi / NFFT)
    return (jnp.cos(angle), jnp.sin(angle))

def shifted_stack(masked, keep):
    lead = LAGS_T // 2
    side = LAGS_X // 2
    padded = jnp.pad(masked, ((lead, lead), (0, 0), (side, side)))
    height = masked.shape[0]
    width = masked.shape[2]
    pieces = [padded[LAGS_T - 1 - a:LAGS_T - 1 - a + height, :, LAGS_X - 1 - b:LAGS_X - 1 - b + width] for a in range(LAGS_T) for b in range(LAGS_X)]
    return jnp.stack(pieces) * keep[None, :, None, None]

def solve_filter(gram, rhs, damping):
    count = gram.shape[0]
    centre = LAGS_T // 2 * LAGS_X + LAGS_X // 2
    unit = (jnp.arange(count) == centre).astype(jnp.float32)
    eye = jnp.eye(count, dtype=jnp.float32)
    factor = jnp.linalg.cholesky(gram + damping * eye)
    return jax.scipy.linalg.cho_solve((factor, True), rhs + damping * unit)

def fill_panel(data, recip, gap, owner):
    blocks = data.reshape(2, NF, RECV, N_SRC, K_DEV)
    pieces = recip.reshape(2, NF, RECV, N_SRC, NEAR)
    filled = jnp.zeros_like(pieces).at[:, :, :, owner, :].set(pieces)
    missing = (gap.reshape(RECV, N_SRC, NEAR) == 1)[None, None]
    near = jnp.where(missing, filled, blocks[..., :NEAR])
    blocks = jnp.concatenate([near, blocks[..., NEAR:]], axis=4)
    return blocks.reshape(2, NF, RECV, KTOT)

def reference(data, recip, gap, owner, weights, start_row, end_row, recorded):
    panel = fill_panel(data, recip, gap, owner)

    def one_freq(pair):
        left, right = pair
        real = jnp.dot(left[0].astype(jnp.float32), right[0].astype(jnp.float32), preferred_element_type=jnp.float32) - jnp.dot(left[1].astype(jnp.float32), right[1].astype(jnp.float32), preferred_element_type=jnp.float32)
        imag = jnp.dot(left[0].astype(jnp.float32), right[1].astype(jnp.float32), preferred_element_type=jnp.float32) + jnp.dot(left[1].astype(jnp.float32), right[0].astype(jnp.float32), preferred_element_type=jnp.float32)
        return (real, imag)
    real, imag = lax.map(one_freq, (jnp.moveaxis(panel, 1, 0), jnp.moveaxis(weights, 1, 0)))
    cosine, sine = phase_tables(jnp.arange(NT, dtype=jnp.int32), jnp.arange(NF, dtype=jnp.int32))
    hp = lax.Precision.HIGHEST
    trace = (jnp.einsum('tf,frs->tsr', cosine, real, precision=hp) - jnp.einsum('tf,frs->tsr', sine, imag, precision=hp)) * (1.0 / math.sqrt(NF))
    padded = jnp.pad(trace, ((HALO, HALO), (0, 0), (0, 0)))
    damping = float(WROWS * SOUT * RECV)

    def one_window(index):
        ext = lax.dynamic_slice_in_dim(padded, index * T_DEV, WROWS, 0)
        rows = index * T_DEV - HALO + jnp.arange(WROWS, dtype=jnp.int32)
        keep = ((rows >= start_row[index]) & (rows < end_row[index])).astype(jnp.float32)
        target = lax.dynamic_slice_in_dim(recorded, index * WROWS, WROWS, 0).astype(jnp.float32) * keep[:, None, None]
        stack = shifted_stack(ext * keep[:, None, None], keep)
        flat = stack.reshape(NU, -1)
        gram = jnp.dot(flat, flat.T, precision=hp)
        rhs = jnp.dot(flat, target.reshape(-1), precision=hp)
        filt = solve_filter(gram, rhs, damping)
        matched = jnp.einsum('u,uwsr->wsr', filt, stack, precision=hp)
        return (target - matched, filt)
    prim, filters = lax.map(one_window, jnp.arange(N_FREQ, dtype=jnp.int32))
    primaries = prim.reshape(N_FREQ * WROWS, SOUT, RECV).astype(jnp.bfloat16)
    return (primaries, filters)
```

```python
import functools
import math

import jax
import jax.numpy as jnp
from jax import lax
from jax.experimental import pallas as pl
from jax.experimental.pallas import tpu as pltpu
from jax.sharding import PartitionSpec as P

RECV = 128
NFFT = 512
F_LOW = 40
NEAR = 16
HALO = 8
LAGS_T = 9
LAGS_X = 3
NU = LAGS_T * LAGS_X
NP = 32
CHUNKS = 4
F32 = jnp.float32
BF16 = jnp.bfloat16


def hdot(a, b, dims=((1,), (0,))):
    return lax.dot_general(
        a, b, (dims, ((), ())), precision=lax.Precision.HIGHEST, preferred_element_type=F32
    )


def bdot(a, b):
    return jnp.dot(a, b, preferred_element_type=F32)


def iota(shape, dim):
    return lax.broadcasted_iota(jnp.int32, shape, dim)


def third(n):
    return (n * 171) >> 9


def kernel(
    nsrc, nfreq, comps, total_out, scale,
    data, recip, gap, owner, weights, start, end, recorded,
    prim, filt,
    dbuf, wbuf, rin, gin, recb, rbuf, pout, pbuf, gath, shifts, rec32, zbuf, hbig,
    lsem, dsem, rsend, rrecv, psend, precv, gsend, grecv, zsend, zrecv,
):
    me = lax.axis_index("src")
    here = lax.axis_index("freq")
    depth = data.shape[3]
    wrows = recorded.shape[0]
    outs = recorded.shape[1]
    step = depth // CHUNKS
    sout = total_out
    log_c = comps.bit_length() - 1
    k3 = LAGS_X * comps

    local = [
        pltpu.make_async_copy(recip, rin, lsem.at[0]),
        pltpu.make_async_copy(gap, gin, lsem.at[1]),
        pltpu.make_async_copy(recorded, recb, lsem.at[2]),
    ]
    for copy in local:
        copy.start()
    big = []
    for i in range(CHUNKS):
        cut = pl.ds(i * step, step)
        big.append(
            (
                pltpu.make_async_copy(data.at[:, :, :, cut], dbuf.at[:, :, :, cut], dsem.at[2 * i]),
                pltpu.make_async_copy(weights.at[:, :, cut, :], wbuf.at[:, :, cut, :], dsem.at[2 * i + 1]),
            )
        )
        for copy in big[-1]:
            copy.start()

    src_peers = [lax.rem(me + k, nsrc) for k in range(1, nsrc)]
    freq_peers = [lax.rem(here + k, nfreq) for k in range(1, nfreq)]
    barrier = pltpu.get_barrier_semaphore()
    for peer in src_peers:
        pl.semaphore_signal(barrier, inc=1, device_id={"src": peer}, device_id_type=pl.DeviceIdType.MESH)
    for peer in freq_peers:
        pl.semaphore_signal(barrier, inc=1, device_id={"freq": peer}, device_id_type=pl.DeviceIdType.MESH)

    def exchange(axis, mine, peers, src_of, buf, rows, send, recv):
        slot = buf.at[pl.ds(pl.multiple_of(mine * rows, rows), rows), :]
        copies = []
        for k, peer in enumerate(peers):
            copies.append(
                pltpu.make_async_remote_copy(
                    src_ref=src_of(peer),
                    dst_ref=slot,
                    send_sem=send.at[k],
                    recv_sem=recv.at[k],
                    device_id={axis: peer},
                    device_id_type=pl.DeviceIdType.MESH,
                )
            )
            copies[-1].start()
        return copies

    local[0].wait()
    for i in range(2):
        flipped = rin[i, 0].astype(F32).T.astype(BF16)
        rbuf[pl.ds(pl.multiple_of(me * 2 * NEAR + i * NEAR, NEAR), NEAR), :] = flipped
    pl.semaphore_wait(barrier, nsrc - 1 + nfreq - 1)
    own = rbuf.at[pl.ds(pl.multiple_of(me * 2 * NEAR, 2 * NEAR), 2 * NEAR), :]
    sent_r = exchange("src", me, src_peers, lambda peer: own, rbuf, 2 * NEAR, rsend, rrecv)

    local[1].wait()
    missing = gin[...] == 1
    gap_t = jnp.where(missing, 1.0, 0.0).astype(F32).T
    acc0 = jnp.zeros((2 * RECV, sout), F32)
    acc1 = jnp.zeros((2 * RECV, sout), F32)
    for i in range(CHUNKS):
        for copy in big[i]:
            copy.wait()
        if i == 0:
            for ci in range(2):
                head = dbuf[ci, 0, :, :NEAR].astype(F32)
                dbuf[ci, 0, :, :NEAR] = jnp.where(missing, 0.0, head).astype(BF16)
        cut = slice(i * step, (i + 1) * step)
        left = dbuf[:, 0, :, cut].reshape(2 * RECV, step)
        acc0 = acc0 + bdot(left, wbuf[0, 0, cut, :])
        acc1 = acc1 + bdot(left, wbuf[1, 0, cut, :])
    real = (acc0[:RECV] - acc1[RECV:]).T
    imag = (acc1[:RECV] + acc0[RECV:]).T

    near_w = [wbuf[ci, 0, :NEAR, :].astype(F32).T.astype(BF16) for ci in range(2)]
    for copy in sent_r:
        copy.wait()
    near = []
    for ci in range(2):
        total = jnp.zeros((NEAR, RECV), F32)
        for j in range(nsrc):
            pick = jnp.where(owner[j] == me, 1.0, 0.0).astype(F32)
            total = total + rbuf[j * 2 * NEAR + ci * NEAR : j * 2 * NEAR + (ci + 1) * NEAR, :].astype(F32) * pick
        near.append((total * gap_t).astype(BF16))
    real = real + bdot(near_w[0], near[0]) - bdot(near_w[1], near[1])
    imag = imag + bdot(near_w[0], near[1]) + bdot(near_w[1], near[0])

    span = 2 * outs
    for d in range(nsrc):
        pout[d * span : d * span + outs, :] = real[d * outs : (d + 1) * outs]
        pout[d * span + outs : (d + 1) * span, :] = imag[d * outs : (d + 1) * outs]

    def block_for(peer):
        return pout.at[pl.ds(pl.multiple_of(peer * span, span), span), :]

    sent_p = exchange("src", me, src_peers, block_for, pbuf, span, psend, precv)
    mine = pl.ds(pl.multiple_of(me * span, span), span)
    pbuf[mine, :] = pout[mine, :]

    base = here * (wrows - 2 * HALO) - HALO
    first, last = start[0], end[0]

    def delayed(u, c, n):
        t = base + u
        v = t - (third(n) - LAGS_T // 2)
        valid = (t >= first) & (t < last) & (v >= first) & (v < last) & (n < NU)
        turns = ((F_LOW + (c >> 1)) * v + (NFFT // 4) * (c & 1)) & (NFFT - 1)
        return jnp.where(valid, jnp.cos(turns.astype(F32) * (2.0 * math.pi / NFFT)) * scale, 0.0)

    rows_cn = comps * NP
    shape = (rows_cn, 128)
    row = iota(shape, 0)
    u_t = delayed(iota(shape, 1), row >> 5, row & (NP - 1))
    shape = (wrows, rows_cn)
    lane = iota(shape, 1)
    u_n = delayed(iota(shape, 0), lane >> 5, lane & (NP - 1))
    shape = (128, 128)
    for c in range(comps):
        block = delayed(iota(shape, 0), c, iota(shape, 1))
        hbig[:, c * 128 : (c + 1) * 128] = hdot(u_t, block)
    shape = (rows_cn, k3)
    row, lane = iota(shape, 0), iota(shape, 1)
    n = row & (NP - 1)
    same = ((lane >> log_c) == n - 3 * third(n)) & ((lane & (comps - 1)) == (row >> 5)) & (n < NU)
    pick_rows = jnp.where(same, 1.0, 0.0).astype(F32)

    local[2].wait()
    rec32[...] = recb[...].astype(F32).reshape(wrows * outs, RECV)

    for copy in sent_p:
        copy.wait()
    pred = pbuf[0:span, :]
    for j in range(1, nsrc):
        pred = pred + pbuf[j * span : (j + 1) * span, :]
    mine = pl.ds(pl.multiple_of(here * span, span), span)
    gath[mine, :] = pred
    sent_g = exchange("freq", here, freq_peers, lambda peer: gath.at[mine, :], gath, span, gsend, grecv)
    for copy in sent_g:
        copy.wait()

    size = comps * outs
    whole = gath[...]
    lane = iota((size, RECV), 1)
    shifts[0:size, :] = jnp.where(lane == RECV - 1, 0.0, pltpu.roll(whole, RECV - 1, 1))
    shifts[size : 2 * size, :] = whole
    shifts[2 * size :, :] = jnp.where(lane == 0, 0.0, pltpu.roll(whole, 1, 1))
    waves = jnp.concatenate([shifts[pl.ds(s, k3, stride=outs), :] for s in range(outs)], axis=1)
    trace = jnp.concatenate([rec32[pl.ds(s, wrows, stride=outs), :] for s in range(outs)], axis=1)

    qw = zbuf.shape[1] - 128
    slot = pl.ds(pl.multiple_of(me * k3, k3), k3)
    zbuf[slot, 0:k3] = hdot(waves, waves, ((1,), (1,)))
    zbuf[slot, qw : qw + wrows] = hdot(waves, trace, ((1,), (1,)))
    sent_z = exchange("src", me, src_peers, lambda peer: zbuf.at[slot, :], zbuf, k3, zsend, zrecv)
    for copy in sent_z:
        copy.wait()
    both = zbuf[0:k3, :]
    for j in range(1, nsrc):
        both = both + zbuf[j * k3 : (j + 1) * k3, :]
    lane = iota((k3, 128), 1)
    corr = both[:, 0:k3]
    cross = jnp.where(lane < wrows, both[:, qw:], 0.0)

    wide = hdot(pick_rows, corr)
    gram = jnp.zeros((NP, 128), F32)
    shape = (k3, 128)
    row, lane = iota(shape, 0), iota(shape, 1)
    lag = lane - 3 * third(lane)
    for c in range(comps):
        same = ((row >> log_c) == lag) & ((row & (comps - 1)) == c) & (lane < NU)
        grid = hdot(wide, jnp.where(same, 1.0, 0.0).astype(F32)) * hbig[:, c * 128 : (c + 1) * 128]
        for d in range(comps):
            gram = gram + grid[d * NP : (d + 1) * NP]
    spread = hdot(pick_rows, cross) * u_t
    right = jnp.zeros((NP, 128), F32)
    for d in range(comps):
        right = right + spread[d * NP : (d + 1) * NP]
    right = jnp.sum(right, axis=1, keepdims=True)

    damping = float(wrows * total_out * RECV)
    shape = (NP, 128)
    row, lane = iota(shape, 0), iota(shape, 1)
    centre = LAGS_T // 2 * LAGS_X + LAGS_X // 2
    right = right + jnp.where(row == centre, damping, 0.0)
    system = jnp.where(lane == 127, right, gram + jnp.where(row == lane, damping, 0.0))
    for k in range(NU):
        pivot = system[k : k + 1, :] * (1.0 / system[k : k + 1, k : k + 1])
        system = jnp.where(row == k, pivot, system - system[:, k : k + 1] * pivot)
    coef = system[:, 127:128]
    spread = jnp.sum(jnp.where(row == lane, coef, 0.0), axis=0, keepdims=True)
    filt[...] = spread[:, :NU]

    weighted = pick_rows * jnp.concatenate([coef] * comps, axis=0)
    mix = hdot(u_n, weighted)
    matched = hdot(mix, waves)
    t = base + iota((wrows, 1), 0)
    keep = jnp.where((t >= first) & (t < last), 1.0, 0.0).astype(F32)
    prim[...] = ((trace - matched) * keep).astype(BF16)


def solution(mesh):
    nsrc, nfreq = mesh.shape["src"], mesh.shape["freq"]

    def body(data, recip, gap, owner, weights, start_row, end_row, recorded):
        assert data.shape[1] == 1
        wrows, outs, recv = recorded.shape
        comps = 2 * nfreq
        k3 = LAGS_X * comps
        zlanes = -(-k3 // 128) * 128 + 128
        sout = weights.shape[3]
        anywhere = pl.BlockSpec(memory_space=pl.ANY)
        scalar = pl.BlockSpec(memory_space=pltpu.SMEM)
        vmem = pl.BlockSpec(memory_space=pltpu.VMEM)
        dma = pltpu.SemaphoreType.DMA
        primaries, filters = pl.pallas_call(
            functools.partial(kernel, nsrc, nfreq, comps, sout, 1.0 / math.sqrt(nfreq)),
            out_shape=(
                jax.ShapeDtypeStruct((wrows, outs * recv), BF16),
                jax.ShapeDtypeStruct((1, NU), F32),
            ),
            in_specs=[anywhere, anywhere, anywhere, scalar, anywhere, scalar, scalar, anywhere],
            out_specs=(vmem, vmem),
            scratch_shapes=[
                pltpu.VMEM(data.shape, BF16),
                pltpu.VMEM(weights.shape, BF16),
                pltpu.VMEM(recip.shape, BF16),
                pltpu.VMEM(gap.shape, jnp.int32),
                pltpu.VMEM(recorded.shape, BF16),
                pltpu.VMEM((nsrc * 2 * NEAR, recv), BF16),
                pltpu.VMEM((nsrc * 2 * outs, recv), F32),
                pltpu.VMEM((nsrc * 2 * outs, recv), F32),
                pltpu.VMEM((comps * outs, recv), F32),
                pltpu.VMEM((k3 * outs, recv), F32),
                pltpu.VMEM((wrows * outs, recv), F32),
                pltpu.VMEM((nsrc * k3, zlanes), F32),
                pltpu.VMEM((comps * NP, comps * 128), F32),
                dma((3,)),
                dma((2 * CHUNKS,)),
                dma((nsrc,)), dma((nsrc,)),
                dma((nsrc,)), dma((nsrc,)),
                dma((nfreq,)), dma((nfreq,)),
                dma((nsrc,)), dma((nsrc,)),
            ],
            compiler_params=pltpu.CompilerParams(
                collective_id=0, has_side_effects=True, vmem_limit_bytes=56 * 1024 * 1024
            ),
            name="multiples",
        )(data, recip, gap, owner, weights, start_row, end_row, recorded)
        return primaries.reshape(wrows, outs, recv), filters

    placed = (
        P(None, "freq", None, "src"),
        P(None, "freq", None, "src"),
        P(None, "src"),
        P(),
        P(None, "freq", "src", None),
        P("freq"),
        P("freq"),
        P("freq", "src", None),
    )
    return jax.shard_map(
        body,
        mesh=mesh,
        in_specs=placed,
        out_specs=(P("freq", "src", None), P("freq", None)),
        check_vma=False,
    )
```

```python
import functools
import math

import jax
import jax.numpy as jnp
from jax import lax
from jax.experimental import pallas as pl
from jax.experimental.pallas import tpu as pltpu
from jax.sharding import PartitionSpec as P

RECV = 128
NFFT = 512
F_LOW = 40
NEAR = 16
HALO = 8
LAGS_T = 9
LAGS_X = 3
NU = LAGS_T * LAGS_X
NP = 32
CHUNKS = 4
F32 = jnp.float32
BF16 = jnp.bfloat16


def hdot(a, b, dims=((1,), (0,))):
    return lax.dot_general(
        a, b, (dims, ((), ())), precision=lax.Precision.HIGHEST, preferred_element_type=F32
    )


def bdot(a, b):
    return jnp.dot(a, b, preferred_element_type=F32)


def iota(shape, dim):
    return lax.broadcasted_iota(jnp.int32, shape, dim)


def split3(x):
    high = x.astype(BF16).astype(F32)
    rest = x - high
    middle = rest.astype(BF16).astype(F32)
    return high, middle, rest - middle


def cosine(turns):
    y = (turns - NFFT // 2).astype(F32) * (math.pi / NFFT)
    square = y * y
    series = jnp.full_like(y, 1.0 / 6227020800.0)
    for factor in (-1.0 / 39916800.0, 1.0 / 362880.0, -1.0 / 5040.0, 1.0 / 120.0, -1.0 / 6.0, 1.0):
        series = series * square + factor
    sine = series * y
    return 2.0 * sine * sine - 1.0


def third(n):
    return (n * 171) >> 9


def kernel(
    nsrc, nfreq, comps, total_out, scale,
    data, recip, gap, owner, weights, start, end, recorded,
    prim, filt,
    dbuf, wbuf, rin, gin, recb, rbuf, pout, pbuf, gath, shifts, rec32, zbuf, hbig,
    lsem, dsem, rsend, rrecv, psend, precv, gsend, grecv, zsend, zrecv,
):
    me = lax.axis_index("src")
    here = lax.axis_index("freq")
    depth = data.shape[3]
    wrows = recorded.shape[0]
    outs = recorded.shape[1]
    step = depth // CHUNKS
    sout = total_out
    log_c = comps.bit_length() - 1
    k3 = LAGS_X * comps

    local = [
        pltpu.make_async_copy(recip, rin, lsem.at[0]),
        pltpu.make_async_copy(gap, gin, lsem.at[1]),
        pltpu.make_async_copy(recorded, recb, lsem.at[2]),
    ]
    for copy in local:
        copy.start()
    big = []
    for i in range(CHUNKS):
        cut = pl.ds(i * step, step)
        big.append(
            (
                pltpu.make_async_copy(data.at[:, :, :, cut], dbuf.at[:, :, :, cut], dsem.at[2 * i]),
                pltpu.make_async_copy(weights.at[:, :, :, cut], wbuf.at[:, :, :, cut], dsem.at[2 * i + 1]),
            )
        )
        for copy in big[-1]:
            copy.start()

    src_peers = [lax.rem(me + k, nsrc) for k in range(1, nsrc)]
    freq_peers = [lax.rem(here + k, nfreq) for k in range(1, nfreq)]
    barrier = pltpu.get_barrier_semaphore()
    for peer in src_peers:
        pl.semaphore_signal(barrier, inc=1, device_id={"src": peer}, device_id_type=pl.DeviceIdType.MESH)
    for peer in freq_peers:
        pl.semaphore_signal(barrier, inc=1, device_id={"freq": peer}, device_id_type=pl.DeviceIdType.MESH)

    def exchange(axis, mine, peers, src_of, buf, rows, send, recv):
        slot = buf.at[pl.ds(pl.multiple_of(mine * rows, rows), rows), :]
        copies = []
        for k, peer in enumerate(peers):
            copies.append(
                pltpu.make_async_remote_copy(
                    src_ref=src_of(peer),
                    dst_ref=slot,
                    send_sem=send.at[k],
                    recv_sem=recv.at[k],
                    device_id={axis: peer},
                    device_id_type=pl.DeviceIdType.MESH,
                )
            )
            copies[-1].start()
        return copies

    local[0].wait()
    mine = pl.ds(pl.multiple_of(me * 2 * NEAR, 2 * NEAR), 2 * NEAR)
    rbuf[mine, :] = rin[...].reshape(2 * NEAR, RECV)
    pl.semaphore_wait(barrier, nsrc - 1 + nfreq - 1)
    sent_r = exchange("src", me, src_peers, lambda peer: rbuf.at[mine, :], rbuf, 2 * NEAR, rsend, rrecv)

    local[1].wait()
    gap_t = jnp.where(gin[...] == 1, 1.0, 0.0).astype(F32)
    present = 1.0 - gap_t.T
    acc = jnp.zeros((2 * sout, 2 * RECV), F32)
    for i in range(CHUNKS):
        for copy in big[i]:
            copy.wait()
        if i == 0:
            for ci in range(2):
                head = dbuf[ci, 0, :, :NEAR].astype(F32)
                dbuf[ci, 0, :, :NEAR] = jnp.where(present > 0.5, head, 0.0).astype(BF16)
        cut = slice(i * step, (i + 1) * step)
        left = wbuf[:, 0, :, cut].reshape(2 * sout, step)
        right = dbuf[:, 0, :, cut].reshape(2 * RECV, step)
        acc = acc + lax.dot_general(left, right, (((1,), (1,)), ((), ())), preferred_element_type=F32)

    near_w = wbuf[:, 0, :, :NEAR].reshape(2 * sout, NEAR)
    for copy in sent_r:
        copy.wait()
    near = []
    for ci in range(2):
        total = jnp.zeros((NEAR, RECV), F32)
        for j in range(nsrc):
            pick = jnp.where(owner[j] == me, 1.0, 0.0).astype(F32)
            total = total + rbuf[j * 2 * NEAR + ci * NEAR : j * 2 * NEAR + (ci + 1) * NEAR, :].astype(F32) * pick
        near.append((total * gap_t).astype(BF16))
    acc = acc + bdot(near_w, jnp.concatenate(near, axis=1))
    real = acc[:sout, :RECV] - acc[sout:, RECV:]
    imag = acc[sout:, :RECV] + acc[:sout, RECV:]

    span = 2 * outs
    for d in range(nsrc):
        pout[d * span : d * span + outs, :] = real[d * outs : (d + 1) * outs]
        pout[d * span + outs : (d + 1) * span, :] = imag[d * outs : (d + 1) * outs]

    def block_for(peer):
        return pout.at[pl.ds(pl.multiple_of(peer * span, span), span), :]

    sent_p = exchange("src", me, src_peers, block_for, pbuf, span, psend, precv)
    mine = pl.ds(pl.multiple_of(me * span, span), span)
    pbuf[mine, :] = pout[mine, :]

    base = here * (wrows - 2 * HALO) - HALO
    first, last = start[0], end[0]

    def delayed(u, c, n):
        t = base + u
        v = t - (third(n) - LAGS_T // 2)
        valid = (t >= first) & (t < last) & (v >= first) & (v < last) & (n < NU)
        turns = ((F_LOW + (c >> 1)) * v + (NFFT // 4) * (c & 1)) & (NFFT - 1)
        return jnp.where(valid, cosine(turns) * scale, 0.0)

    rows_cn = comps * NP
    shape = (rows_cn, 128)
    row = iota(shape, 0)
    u_t = delayed(iota(shape, 1), row >> 5, row & (NP - 1))
    shape = (wrows, rows_cn)
    lane = iota(shape, 1)
    u_n = delayed(iota(shape, 0), lane >> 5, lane & (NP - 1))
    shape = (rows_cn, 3 * k3)
    row, lane = iota(shape, 0), iota(shape, 1)
    lane = jnp.where(lane >= 2 * k3, lane - 2 * k3, jnp.where(lane >= k3, lane - k3, lane))
    n = row & (NP - 1)
    same = ((lane >> log_c) == n - 3 * third(n)) & ((lane & (comps - 1)) == (row >> 5)) & (n < NU)
    pick_rows = jnp.where(same, 1.0, 0.0).astype(F32)
    shape = (k3, rows_cn)
    row, lane = iota(shape, 0), iota(shape, 1)
    n = lane & (NP - 1)
    same = ((row >> log_c) == n - 3 * third(n)) & ((row & (comps - 1)) == (lane >> 5)) & (n < NU)
    pick_lanes = jnp.where(same, 1.0, 0.0).astype(BF16)

    local[2].wait()
    rec32[...] = recb[...].astype(F32).reshape(wrows * outs, RECV)
    trace = jnp.concatenate([rec32[pl.ds(s, wrows, stride=outs), :] for s in range(outs)], axis=1)

    for copy in sent_p:
        copy.wait()
    pred = pbuf[0:span, :]
    for j in range(1, nsrc):
        pred = pred + pbuf[j * span : (j + 1) * span, :]
    mine = pl.ds(pl.multiple_of(here * span, span), span)
    gath[mine, :] = pred
    sent_g = exchange("freq", here, freq_peers, lambda peer: gath.at[mine, :], gath, span, gsend, grecv)
    hbig[...] = hdot(u_t[:, :wrows], u_n)
    for copy in sent_g:
        copy.wait()

    size = comps * outs
    whole = gath[...]
    lane = iota((size, RECV), 1)
    shifts[0:size, :] = jnp.where(lane == RECV - 1, 0.0, pltpu.roll(whole, RECV - 1, 1))
    shifts[size : 2 * size, :] = whole
    shifts[2 * size :, :] = jnp.where(lane == 0, 0.0, pltpu.roll(whole, 1, 1))
    waves = jnp.concatenate([shifts[pl.ds(s, k3, stride=outs), :] for s in range(outs)], axis=1)

    parts = split3(waves)
    stacked = jnp.concatenate([*parts, trace], axis=0).astype(BF16)
    waves3 = stacked[: 3 * k3]
    pair = lax.dot_general(waves3, stacked, (((1,), (1,)), ((), ())), preferred_element_type=F32)
    pair = pair[:k3] + pair[k3 : 2 * k3] + pair[2 * k3 :]
    slot = pl.ds(pl.multiple_of(me * k3, k3), k3)
    zused = 3 * k3 + wrows
    zbuf[slot, 0:zused] = pair
    sent_z = exchange("src", me, src_peers, lambda peer: zbuf.at[slot, :], zbuf, k3, zsend, zrecv)
    for copy in sent_z:
        copy.wait()
    both = zbuf[0:k3, :]
    for j in range(1, nsrc):
        both = both + zbuf[j * k3 : (j + 1) * k3, :]
    corr = both[:, 0:k3] + both[:, k3 : 2 * k3] + both[:, 2 * k3 : 3 * k3]
    cross = both[:, 3 * k3 : zused]

    corr3 = jnp.concatenate(split3(corr), axis=0).astype(BF16)
    cross3 = jnp.concatenate(split3(cross), axis=0).astype(BF16)
    pick_bf = pick_rows.astype(BF16)
    grid = bdot(pick_bf, bdot(corr3, pick_lanes).astype(BF16)) * hbig[...]
    spread = bdot(pick_bf, cross3) * u_t[:, :wrows]
    gram = grid[:NP]
    right = spread[:NP]
    for d in range(1, comps):
        gram = gram + grid[d * NP : (d + 1) * NP]
        right = right + spread[d * NP : (d + 1) * NP]
    tiles = gram[:, :128]
    for d in range(1, rows_cn // 128):
        tiles = tiles + gram[:, d * 128 : (d + 1) * 128]
    tiles = tiles + pltpu.roll(tiles, 64, 1)
    tiles = tiles + pltpu.roll(tiles, 32, 1)
    right = jnp.sum(right, axis=1, keepdims=True)

    damping = float(wrows * total_out * RECV)
    shape = (NP, 128)
    row, lane = iota(shape, 0), iota(shape, 1)
    centre = LAGS_T // 2 * LAGS_X + LAGS_X // 2
    right = right + jnp.where(row == centre, damping, 0.0)
    system = jnp.where(lane == 127, right, tiles + jnp.where(row == lane, damping, 0.0))
    for k in range(0, NU, 3):
        cols = [jnp.broadcast_to(system[:, k + i : k + i + 1], (NP, 128)) for i in range(3)]
        rows = [system[k + i : k + i + 1, :] for i in range(3)]
        inner = [[cols[j][k + i : k + i + 1, :] for j in range(3)] for i in range(3)]
        for i in range(3):
            inverse = 1.0 / inner[i][i]
            rows[i] = rows[i] * inverse
            scaled = [None if j <= i else inner[i][j] * inverse for j in range(3)]
            for j in range(3):
                if j > i:
                    rows[j] = rows[j] - inner[j][i] * rows[i]
                    for m in range(i + 1, 3):
                        inner[j][m] = inner[j][m] - inner[j][i] * scaled[m]
            for m in range(i + 1, 3):
                inner[i][m] = scaled[m]
        rows[1] = rows[1] - inner[1][2] * rows[2]
        rows[0] = rows[0] - inner[0][1] * rows[1] - inner[0][2] * rows[2]
        system = system - (cols[0] * rows[0] + cols[1] * rows[1] + cols[2] * rows[2])
        for i in range(3):
            system = jnp.where(row == k + i, rows[i], system)
    coef = system[:, 127:128]
    across = jnp.sum(jnp.where(row == lane, coef, 0.0), axis=0, keepdims=True)
    filt[...] = across[:, :NU]

    weighted = pick_rows * jnp.concatenate([coef] * comps, axis=0)
    mix = jnp.concatenate(split3(hdot(u_n, weighted)), axis=0).astype(BF16)
    matched = bdot(mix, waves3)
    matched = matched[:wrows] + matched[wrows : 2 * wrows] + matched[2 * wrows :]
    t = base + iota((wrows, 1), 0)
    keep = jnp.where((t >= first) & (t < last), 1.0, 0.0).astype(F32)
    prim[...] = ((trace - matched) * keep).astype(BF16)


def solution(mesh):
    nsrc, nfreq = mesh.shape["src"], mesh.shape["freq"]

    def body(data, recip, gap, owner, weights, start_row, end_row, recorded):
        assert data.shape[1] == 1
        wrows, outs, recv = recorded.shape
        comps = 2 * nfreq
        k3 = LAGS_X * comps
        zlanes = -(-(3 * k3 + wrows) // 128) * 128
        recip, weights, gap = recip.swapaxes(2, 3), weights.swapaxes(2, 3), gap.T
        sout = weights.shape[2]
        anywhere = pl.BlockSpec(memory_space=pl.ANY)
        scalar = pl.BlockSpec(memory_space=pltpu.SMEM)
        vmem = pl.BlockSpec(memory_space=pltpu.VMEM)
        dma = pltpu.SemaphoreType.DMA
        primaries, filters = pl.pallas_call(
            functools.partial(kernel, nsrc, nfreq, comps, sout, 1.0 / math.sqrt(nfreq)),
            out_shape=(
                jax.ShapeDtypeStruct((wrows, outs * recv), BF16),
                jax.ShapeDtypeStruct((1, NU), F32),
            ),
            in_specs=[anywhere, anywhere, anywhere, scalar, anywhere, scalar, scalar, anywhere],
            out_specs=(vmem, vmem),
            scratch_shapes=[
                pltpu.VMEM(data.shape, BF16),
                pltpu.VMEM(weights.shape, BF16),
                pltpu.VMEM(recip.shape, BF16),
                pltpu.VMEM(gap.shape, jnp.int32),
                pltpu.VMEM(recorded.shape, BF16),
                pltpu.VMEM((nsrc * 2 * NEAR, recv), BF16),
                pltpu.VMEM((nsrc * 2 * outs, recv), F32),
                pltpu.VMEM((nsrc * 2 * outs, recv), F32),
                pltpu.VMEM((comps * outs, recv), F32),
                pltpu.VMEM((k3 * outs, recv), F32),
                pltpu.VMEM((wrows * outs, recv), F32),
                pltpu.VMEM((nsrc * k3, zlanes), F32),
                pltpu.VMEM((comps * NP, comps * NP), F32),
                dma((3,)),
                dma((2 * CHUNKS,)),
                dma((nsrc,)), dma((nsrc,)),
                dma((nsrc,)), dma((nsrc,)),
                dma((nfreq,)), dma((nfreq,)),
                dma((nsrc,)), dma((nsrc,)),
            ],
            compiler_params=pltpu.CompilerParams(
                collective_id=0, has_side_effects=True, vmem_limit_bytes=56 * 1024 * 1024
            ),
            name="multiples",
        )(data, recip, gap, owner, weights, start_row, end_row, recorded)
        return primaries.reshape(wrows, outs, recv), filters

    placed = (
        P(None, "freq", None, "src"),
        P(None, "freq", None, "src"),
        P(None, "src"),
        P(),
        P(None, "freq", "src", None),
        P("freq"),
        P("freq"),
        P("freq", "src", None),
    )
    return jax.shard_map(
        body,
        mesh=mesh,
        in_specs=placed,
        out_specs=(P("freq", "src", None), P("freq", None)),
        check_vma=False,
    )
```

```python
import functools
import math

import jax
import jax.numpy as jnp
from jax import lax
from jax.experimental import pallas as pl
from jax.experimental.pallas import tpu as pltpu
from jax.sharding import PartitionSpec as P

RECV = 128
NFFT = 512
F_LOW = 40
NEAR = 16
HALO = 8
LAGS_T = 9
LAGS_X = 3
NU = LAGS_T * LAGS_X
NP = 32
CHUNKS = 4
F32 = jnp.float32
BF16 = jnp.bfloat16


def hdot(a, b, dims=((1,), (0,))):
    return lax.dot_general(
        a, b, (dims, ((), ())), precision=lax.Precision.HIGHEST, preferred_element_type=F32
    )


def bdot(a, b):
    return jnp.dot(a, b, preferred_element_type=F32)


def iota(shape, dim):
    return lax.broadcasted_iota(jnp.int32, shape, dim)


def split3(x):
    high = x.astype(BF16).astype(F32)
    rest = x - high
    middle = rest.astype(BF16).astype(F32)
    return high, middle, rest - middle


def cosine(turns):
    y = (turns - NFFT // 2).astype(F32) * (math.pi / NFFT)
    square = y * y
    series = jnp.full_like(y, 1.0 / 6227020800.0)
    for factor in (-1.0 / 39916800.0, 1.0 / 362880.0, -1.0 / 5040.0, 1.0 / 120.0, -1.0 / 6.0, 1.0):
        series = series * square + factor
    sine = series * y
    return 2.0 * sine * sine - 1.0


def third(n):
    return (n * 171) >> 9


def kernel(
    nsrc, nfreq, comps, total_out, scale,
    data, recip, gap, owner, weights, start, end, recorded,
    prim, filt,
    owner_s, start_s, end_s, dbuf, wbuf, rin, gin, recb, rbuf, pout, pbuf, gath, shifts, rec32, zbuf, hbig,
    lsem, dsem, rsend, rrecv, psend, precv, gsend, grecv, zsend, zrecv,
):
    me = lax.axis_index("src")
    here = lax.axis_index("freq")
    depth = data.shape[3]
    wrows = recorded.shape[0]
    outs = recorded.shape[1]
    step = depth // CHUNKS
    sout = total_out
    log_c = comps.bit_length() - 1
    k3 = LAGS_X * comps

    local = [
        pltpu.make_async_copy(recip, rin, lsem.at[0]),
        pltpu.make_async_copy(gap, gin, lsem.at[1]),
        pltpu.make_async_copy(recorded, recb, lsem.at[2]),
        pltpu.make_async_copy(owner, owner_s, lsem.at[3]),
        pltpu.make_async_copy(start, start_s, lsem.at[4]),
        pltpu.make_async_copy(end, end_s, lsem.at[5]),
    ]
    for copy in local:
        copy.start()
    big = []
    for i in range(CHUNKS):
        cut = pl.ds(i * step, step)
        big.append(
            (
                pltpu.make_async_copy(data.at[:, :, :, cut], dbuf.at[:, :, :, cut], dsem.at[2 * i]),
                pltpu.make_async_copy(weights.at[:, :, :, cut], wbuf.at[:, :, :, cut], dsem.at[2 * i + 1]),
            )
        )
        for copy in big[-1]:
            copy.start()

    src_peers = [lax.rem(me + k, nsrc) for k in range(1, nsrc)]
    freq_peers = [lax.rem(here + k, nfreq) for k in range(1, nfreq)]
    barrier = pltpu.get_barrier_semaphore()
    for peer in src_peers:
        pl.semaphore_signal(barrier, inc=1, device_id={"src": peer}, device_id_type=pl.DeviceIdType.MESH)
    for peer in freq_peers:
        pl.semaphore_signal(barrier, inc=1, device_id={"freq": peer}, device_id_type=pl.DeviceIdType.MESH)

    def exchange(axis, mine, peers, src_of, buf, rows, send, recv):
        slot = buf.at[pl.ds(pl.multiple_of(mine * rows, rows), rows), :]
        copies = []
        for k, peer in enumerate(peers):
            copies.append(
                pltpu.make_async_remote_copy(
                    src_ref=src_of(peer),
                    dst_ref=slot,
                    send_sem=send.at[k],
                    recv_sem=recv.at[k],
                    device_id={axis: peer},
                    device_id_type=pl.DeviceIdType.MESH,
                )
            )
            copies[-1].start()
        return copies

    local[0].wait()
    mine = pl.ds(pl.multiple_of(me * 2 * NEAR, 2 * NEAR), 2 * NEAR)
    rbuf[mine, :] = rin[...].reshape(2 * NEAR, RECV)
    pl.semaphore_wait(barrier, nsrc - 1 + nfreq - 1)
    sent_r = exchange("src", me, src_peers, lambda peer: rbuf.at[mine, :], rbuf, 2 * NEAR, rsend, rrecv)

    local[1].wait()
    gap_t = jnp.where(gin[...] == 1, 1.0, 0.0).astype(F32)
    present = 1.0 - gap_t.T
    acc = jnp.zeros((2 * sout, 2 * RECV), F32)
    for i in range(CHUNKS):
        for copy in big[i]:
            copy.wait()
        if i == 0:
            for ci in range(2):
                head = dbuf[ci, 0, :, :NEAR].astype(F32)
                dbuf[ci, 0, :, :NEAR] = jnp.where(present > 0.5, head, 0.0).astype(BF16)
        cut = slice(i * step, (i + 1) * step)
        left = wbuf[:, 0, :, cut].reshape(2 * sout, step)
        right = dbuf[:, 0, :, cut].reshape(2 * RECV, step)
        acc = acc + lax.dot_general(left, right, (((1,), (1,)), ((), ())), preferred_element_type=F32)

    near_w = wbuf[:, 0, :, :NEAR].reshape(2 * sout, NEAR)
    for copy in sent_r:
        copy.wait()
    local[3].wait()
    near = []
    for ci in range(2):
        total = jnp.zeros((NEAR, RECV), F32)
        for j in range(nsrc):
            pick = jnp.where(owner_s[j] == me, 1.0, 0.0).astype(F32)
            total = total + rbuf[j * 2 * NEAR + ci * NEAR : j * 2 * NEAR + (ci + 1) * NEAR, :].astype(F32) * pick
        near.append((total * gap_t).astype(BF16))
    acc = acc + bdot(near_w, jnp.concatenate(near, axis=1))
    real = acc[:sout, :RECV] - acc[sout:, RECV:]
    imag = acc[sout:, :RECV] + acc[:sout, RECV:]

    span = 2 * outs
    for d in range(nsrc):
        pout[d * span : d * span + outs, :] = real[d * outs : (d + 1) * outs]
        pout[d * span + outs : (d + 1) * span, :] = imag[d * outs : (d + 1) * outs]

    def block_for(peer):
        return pout.at[pl.ds(pl.multiple_of(peer * span, span), span), :]

    sent_p = exchange("src", me, src_peers, block_for, pbuf, span, psend, precv)
    mine = pl.ds(pl.multiple_of(me * span, span), span)
    pbuf[mine, :] = pout[mine, :]

    base = here * (wrows - 2 * HALO) - HALO
    local[4].wait()
    local[5].wait()
    first, last = start_s[0], end_s[0]

    def delayed(u, c, n):
        t = base + u
        v = t - (third(n) - LAGS_T // 2)
        valid = (t >= first) & (t < last) & (v >= first) & (v < last) & (n < NU)
        turns = ((F_LOW + (c >> 1)) * v + (NFFT // 4) * (c & 1)) & (NFFT - 1)
        return jnp.where(valid, cosine(turns) * scale, 0.0)

    rows_cn = comps * NP
    shape = (rows_cn, 128)
    row = iota(shape, 0)
    u_t = delayed(iota(shape, 1), row >> 5, row & (NP - 1))
    shape = (wrows, rows_cn)
    lane = iota(shape, 1)
    u_n = delayed(iota(shape, 0), lane >> 5, lane & (NP - 1))
    shape = (rows_cn, 3 * k3)
    row, lane = iota(shape, 0), iota(shape, 1)
    lane = jnp.where(lane >= 2 * k3, lane - 2 * k3, jnp.where(lane >= k3, lane - k3, lane))
    n = row & (NP - 1)
    same = ((lane >> log_c) == n - 3 * third(n)) & ((lane & (comps - 1)) == (row >> 5)) & (n < NU)
    pick_rows = jnp.where(same, 1.0, 0.0).astype(F32)
    shape = (k3, rows_cn)
    row, lane = iota(shape, 0), iota(shape, 1)
    n = lane & (NP - 1)
    same = ((row >> log_c) == n - 3 * third(n)) & ((row & (comps - 1)) == (lane >> 5)) & (n < NU)
    pick_lanes = jnp.where(same, 1.0, 0.0).astype(BF16)

    local[2].wait()
    rec32[...] = recb[...].astype(F32).reshape(wrows * outs, RECV)
    trace = jnp.concatenate([rec32[pl.ds(s, wrows, stride=outs), :] for s in range(outs)], axis=1)

    for copy in sent_p:
        copy.wait()
    pred = pbuf[0:span, :]
    for j in range(1, nsrc):
        pred = pred + pbuf[j * span : (j + 1) * span, :]
    mine = pl.ds(pl.multiple_of(here * span, span), span)
    gath[mine, :] = pred
    sent_g = exchange("freq", here, freq_peers, lambda peer: gath.at[mine, :], gath, span, gsend, grecv)
    hbig[...] = hdot(u_t[:, :wrows], u_n)
    for copy in sent_g:
        copy.wait()

    size = comps * outs
    whole = gath[...]
    lane = iota((size, RECV), 1)
    shifts[0:size, :] = jnp.where(lane == RECV - 1, 0.0, pltpu.roll(whole, RECV - 1, 1))
    shifts[size : 2 * size, :] = whole
    shifts[2 * size :, :] = jnp.where(lane == 0, 0.0, pltpu.roll(whole, 1, 1))
    waves = jnp.concatenate([shifts[pl.ds(s, k3, stride=outs), :] for s in range(outs)], axis=1)

    parts = split3(waves)
    stacked = jnp.concatenate([*parts, trace], axis=0).astype(BF16)
    waves3 = stacked[: 3 * k3]
    pair = lax.dot_general(waves3, stacked, (((1,), (1,)), ((), ())), preferred_element_type=F32)
    pair = pair[:k3] + pair[k3 : 2 * k3] + pair[2 * k3 :]
    slot = pl.ds(pl.multiple_of(me * k3, k3), k3)
    zused = 3 * k3 + wrows
    zbuf[slot, 0:zused] = pair
    sent_z = exchange("src", me, src_peers, lambda peer: zbuf.at[slot, :], zbuf, k3, zsend, zrecv)
    for copy in sent_z:
        copy.wait()
    both = zbuf[0:k3, :]
    for j in range(1, nsrc):
        both = both + zbuf[j * k3 : (j + 1) * k3, :]
    corr = both[:, 0:k3] + both[:, k3 : 2 * k3] + both[:, 2 * k3 : 3 * k3]
    cross = both[:, 3 * k3 : zused]

    corr3 = jnp.concatenate(split3(corr), axis=0).astype(BF16)
    cross3 = jnp.concatenate(split3(cross), axis=0).astype(BF16)
    pick_bf = pick_rows.astype(BF16)
    grid = bdot(pick_bf, bdot(corr3, pick_lanes).astype(BF16)) * hbig[...]
    spread = bdot(pick_bf, cross3) * u_t[:, :wrows]
    gram = grid[:NP]
    right = spread[:NP]
    for d in range(1, comps):
        gram = gram + grid[d * NP : (d + 1) * NP]
        right = right + spread[d * NP : (d + 1) * NP]
    tiles = gram[:, :128]
    for d in range(1, rows_cn // 128):
        tiles = tiles + gram[:, d * 128 : (d + 1) * 128]
    tiles = tiles + pltpu.roll(tiles, 64, 1)
    tiles = tiles + pltpu.roll(tiles, 32, 1)
    right = jnp.sum(right, axis=1, keepdims=True)

    damping = float(wrows * total_out * RECV)
    shape = (NP, 128)
    row, lane = iota(shape, 0), iota(shape, 1)
    centre = LAGS_T // 2 * LAGS_X + LAGS_X // 2
    right = right + jnp.where(row == centre, damping, 0.0)
    system = jnp.where(lane == 127, right, tiles + jnp.where(row == lane, damping, 0.0))
    for k in range(0, NU, 3):
        cols = [jnp.broadcast_to(system[:, k + i : k + i + 1], (NP, 128)) for i in range(3)]
        rows = [system[k + i : k + i + 1, :] for i in range(3)]
        inner = [[cols[j][k + i : k + i + 1, :] for j in range(3)] for i in range(3)]
        for i in range(3):
            inverse = 1.0 / inner[i][i]
            rows[i] = rows[i] * inverse
            scaled = [None if j <= i else inner[i][j] * inverse for j in range(3)]
            for j in range(3):
                if j > i:
                    rows[j] = rows[j] - inner[j][i] * rows[i]
                    for m in range(i + 1, 3):
                        inner[j][m] = inner[j][m] - inner[j][i] * scaled[m]
            for m in range(i + 1, 3):
                inner[i][m] = scaled[m]
        rows[1] = rows[1] - inner[1][2] * rows[2]
        rows[0] = rows[0] - inner[0][1] * rows[1] - inner[0][2] * rows[2]
        system = system - (cols[0] * rows[0] + cols[1] * rows[1] + cols[2] * rows[2])
        for i in range(3):
            system = jnp.where(row == k + i, rows[i], system)
    coef = system[:, 127:128]
    across = jnp.sum(jnp.where(row == lane, coef, 0.0), axis=0, keepdims=True)
    filt[...] = across[:, :NU]

    weighted = pick_rows * jnp.concatenate([coef] * comps, axis=0)
    mix = jnp.concatenate(split3(hdot(u_n, weighted)), axis=0).astype(BF16)
    matched = bdot(mix, waves3)
    matched = matched[:wrows] + matched[wrows : 2 * wrows] + matched[2 * wrows :]
    t = base + iota((wrows, 1), 0)
    keep = jnp.where((t >= first) & (t < last), 1.0, 0.0).astype(F32)
    result = (trace - matched) * keep
    for s in range(outs):
        rec32[pl.ds(s, wrows, stride=outs), :] = result[:, s * RECV : (s + 1) * RECV]
    prim[...] = rec32[...].astype(BF16)


def finish(prim, filt, prim_out, filt_out, sems):
    copies = [
        pltpu.make_async_copy(prim, prim_out, sems.at[0]),
        pltpu.make_async_copy(filt, filt_out, sems.at[1]),
    ]
    for copy in copies:
        copy.start()
    for copy in copies:
        copy.wait()


def solution(mesh):
    nsrc, nfreq = mesh.shape["src"], mesh.shape["freq"]

    def body(data, recip, gap, owner, weights, start_row, end_row, recorded):
        assert data.shape[1] == 1
        wrows, outs, recv = recorded.shape
        comps = 2 * nfreq
        k3 = LAGS_X * comps
        zlanes = -(-(3 * k3 + wrows) // 128) * 128
        recip, weights, gap = recip.swapaxes(2, 3), weights.swapaxes(2, 3), gap.T
        sout = weights.shape[2]
        anywhere = pl.BlockSpec(memory_space=pltpu.HBM)
        vmem = pl.BlockSpec(memory_space=pltpu.VMEM)
        dma = pltpu.SemaphoreType.DMA
        primaries, filters = pl.pallas_call(
            functools.partial(kernel, nsrc, nfreq, comps, sout, 1.0 / math.sqrt(nfreq)),
            out_shape=(
                jax.ShapeDtypeStruct((wrows * outs, recv), BF16),
                jax.ShapeDtypeStruct((1, NU), F32),
            ),
            in_specs=[anywhere] * 8,
            out_specs=(vmem, vmem),
            scratch_shapes=[
                pltpu.SMEM(owner.shape, jnp.int32),
                pltpu.SMEM(start_row.shape, jnp.int32),
                pltpu.SMEM(end_row.shape, jnp.int32),
                pltpu.VMEM(data.shape, BF16),
                pltpu.VMEM(weights.shape, BF16),
                pltpu.VMEM(recip.shape, BF16),
                pltpu.VMEM(gap.shape, jnp.int32),
                pltpu.VMEM(recorded.shape, BF16),
                pltpu.VMEM((nsrc * 2 * NEAR, recv), BF16),
                pltpu.VMEM((nsrc * 2 * outs, recv), F32),
                pltpu.VMEM((nsrc * 2 * outs, recv), F32),
                pltpu.VMEM((comps * outs, recv), F32),
                pltpu.VMEM((k3 * outs, recv), F32),
                pltpu.VMEM((wrows * outs, recv), F32),
                pltpu.VMEM((nsrc * k3, zlanes), F32),
                pltpu.VMEM((comps * NP, comps * NP), F32),
                dma((6,)),
                dma((2 * CHUNKS,)),
                dma((nsrc,)), dma((nsrc,)),
                dma((nsrc,)), dma((nsrc,)),
                dma((nfreq,)), dma((nfreq,)),
                dma((nsrc,)), dma((nsrc,)),
            ],
            compiler_params=pltpu.CompilerParams(
                collective_id=0, has_side_effects=True, vmem_limit_bytes=56 * 1024 * 1024
            ),
            name="multiples",
        )(data, recip, gap, owner, weights, start_row, end_row, recorded)
        return tuple(
            pl.pallas_call(
                finish,
                out_shape=(
                    jax.ShapeDtypeStruct((wrows, outs, recv), BF16),
                    jax.ShapeDtypeStruct((1, NU), F32),
                ),
                in_specs=[anywhere] * 2,
                out_specs=(anywhere, anywhere),
                scratch_shapes=[dma((2,))],
                compiler_params=pltpu.CompilerParams(vmem_limit_bytes=56 * 1024 * 1024),
                name="finish",
            )(primaries.reshape(wrows, outs, recv), filters)
        )

    placed = (
        P(None, "freq", None, "src"),
        P(None, "freq", None, "src"),
        P(None, "src"),
        P(),
        P(None, "freq", "src", None),
        P("freq"),
        P("freq"),
        P("freq", "src", None),
    )
    return jax.shard_map(
        body,
        mesh=mesh,
        in_specs=placed,
        out_specs=(P("freq", "src", None), P("freq", None)),
        check_vma=False,
    )
```

```python
import functools
import math

import jax
import jax.numpy as jnp
from jax import lax
from jax.experimental import pallas as pl
from jax.experimental.pallas import tpu as pltpu
from jax.sharding import PartitionSpec as P

RECV = 128
NFFT = 512
F_LOW = 40
NEAR = 16
HALO = 8
LAGS_T = 9
LAGS_X = 3
NU = LAGS_T * LAGS_X
NP = 32
CHUNKS = 4
F32 = jnp.float32
BF16 = jnp.bfloat16


def hdot(a, b, dims=((1,), (0,))):
    return lax.dot_general(
        a, b, (dims, ((), ())), precision=lax.Precision.HIGHEST, preferred_element_type=F32
    )


def bdot(a, b):
    return jnp.dot(a, b, preferred_element_type=F32)


def iota(shape, dim):
    return lax.broadcasted_iota(jnp.int32, shape, dim)


def split3(x):
    high = x.astype(BF16).astype(F32)
    rest = x - high
    middle = rest.astype(BF16).astype(F32)
    return high, middle, rest - middle


def cosine(turns):
    y = (turns - NFFT // 2).astype(F32) * (math.pi / NFFT)
    square = y * y
    series = jnp.full_like(y, 1.0 / 6227020800.0)
    for factor in (-1.0 / 39916800.0, 1.0 / 362880.0, -1.0 / 5040.0, 1.0 / 120.0, -1.0 / 6.0, 1.0):
        series = series * square + factor
    sine = series * y
    return 2.0 * sine * sine - 1.0


def third(n):
    return (n * 171) >> 9


def kernel(
    nsrc, nfreq, comps, total_out, scale,
    data, recip, gap, owner, weights, start, end, recorded,
    prim, filt,
    owner_s, start_s, end_s, dbuf, wbuf, rin, gin, recb, nbuf, nacc, pout, pbuf, gath, shifts, rec32, zbuf, hbig,
    lsem, dsem, rsend, rrecv, psend, precv, gsend, grecv, zsend, zrecv,
):
    me = lax.axis_index("src")
    here = lax.axis_index("freq")
    depth = data.shape[3]
    wrows = recorded.shape[0]
    outs = recorded.shape[1]
    step = depth // CHUNKS
    sout = total_out
    log_c = comps.bit_length() - 1
    k3 = LAGS_X * comps

    local = [
        pltpu.make_async_copy(recip, rin, lsem.at[0]),
        pltpu.make_async_copy(gap, gin, lsem.at[1]),
        pltpu.make_async_copy(recorded, recb, lsem.at[2]),
        pltpu.make_async_copy(owner, owner_s, lsem.at[3]),
        pltpu.make_async_copy(start, start_s, lsem.at[4]),
        pltpu.make_async_copy(end, end_s, lsem.at[5]),
    ]
    for copy in local:
        copy.start()
    big = []
    for i in range(CHUNKS):
        cut = pl.ds(i * step, step)
        big.append(
            (
                pltpu.make_async_copy(data.at[:, :, :, cut], dbuf.at[:, :, :, cut], dsem.at[2 * i]),
                pltpu.make_async_copy(weights.at[:, :, :, cut], wbuf.at[:, :, :, cut], dsem.at[2 * i + 1]),
            )
        )
        for copy in big[-1]:
            copy.start()

    src_peers = [lax.rem(me + k, nsrc) for k in range(1, nsrc)]
    freq_peers = [lax.rem(here + k, nfreq) for k in range(1, nfreq)]
    barrier = pltpu.get_barrier_semaphore()
    for peer in src_peers:
        pl.semaphore_signal(barrier, inc=1, device_id={"src": peer}, device_id_type=pl.DeviceIdType.MESH)
    for peer in freq_peers:
        pl.semaphore_signal(barrier, inc=1, device_id={"freq": peer}, device_id_type=pl.DeviceIdType.MESH)

    def exchange(axis, mine, peers, src_of, buf, rows, send, recv):
        slot = buf.at[pl.ds(pl.multiple_of(mine * rows, rows), rows), :]
        copies = []
        for k, peer in enumerate(peers):
            copies.append(
                pltpu.make_async_remote_copy(
                    src_ref=src_of(peer),
                    dst_ref=slot,
                    send_sem=send.at[k],
                    recv_sem=recv.at[k],
                    device_id={axis: peer},
                    device_id_type=pl.DeviceIdType.MESH,
                )
            )
            copies[-1].start()
        return copies

    wrow = 3 * NEAR
    wparts = 2 * sout // 128
    nrows = wrow + wparts * NEAR
    at = pl.multiple_of(me * nrows, NEAR)
    local[0].wait()
    nbuf[pl.ds(at, 2 * NEAR), :] = rin[...].reshape(2 * NEAR, RECV)
    local[1].wait()
    gap_t = jnp.where(gin[...] == 1, 1.0, 0.0).astype(F32)
    nbuf[pl.ds(at + 2 * NEAR, NEAR), :] = gap_t.astype(BF16)
    present = 1.0 - gap_t.T
    for copy in big[0]:
        copy.wait()
    near_w = wbuf[:, 0, :, :NEAR].reshape(2 * sout, NEAR).astype(F32)
    for i in range(wparts):
        nbuf[pl.ds(at + wrow + i * NEAR, NEAR), :] = near_w[i * 128 : (i + 1) * 128].T.astype(BF16)
    pl.semaphore_wait(barrier, nsrc - 1 + nfreq - 1)
    own = nbuf.at[pl.ds(at, nrows), :]
    sent_r = exchange("src", me, src_peers, lambda peer: own, nbuf, nrows, rsend, rrecv)

    acc = jnp.zeros((2 * sout, 2 * RECV), F32)
    for i in range(CHUNKS):
        if i == 0:
            for ci in range(2):
                head = dbuf[ci, 0, :, :NEAR].astype(F32)
                dbuf[ci, 0, :, :NEAR] = jnp.where(present > 0.5, head, 0.0).astype(BF16)
        else:
            for copy in big[i]:
                copy.wait()
        cut = slice(i * step, (i + 1) * step)
        left = wbuf[:, 0, :, cut].reshape(2 * sout, step)
        right = dbuf[:, 0, :, cut].reshape(2 * RECV, step)
        acc = acc + lax.dot_general(left, right, (((1,), (1,)), ((), ())), preferred_element_type=F32)
    real = acc[:sout, :RECV] - acc[sout:, RECV:]
    imag = acc[sout:, :RECV] + acc[:sout, RECV:]

    span = 2 * outs
    for d in range(nsrc):
        pout[d * span : d * span + outs, :] = real[d * outs : (d + 1) * outs]
        pout[d * span + outs : (d + 1) * span, :] = imag[d * outs : (d + 1) * outs]

    def block_for(peer):
        return pout.at[pl.ds(pl.multiple_of(peer * span, span), span), :]

    sent_p = exchange("src", me, src_peers, block_for, pbuf, span, psend, precv)
    mine = pl.ds(pl.multiple_of(me * span, span), span)
    pbuf[mine, :] = pout[mine, :]

    local[2].wait()
    rec32[...] = recb[...].astype(F32).reshape(wrows * outs, RECV)
    trace = jnp.concatenate([rec32[pl.ds(s, wrows, stride=outs), :] for s in range(outs)], axis=1)

    for copy in sent_r:
        copy.wait()
    local[3].wait()
    fills = []
    for b in range(nsrc):
        held = nbuf[b * nrows + 2 * NEAR : b * nrows + 3 * NEAR, :].astype(F32)
        total = jnp.zeros((2 * NEAR, RECV), F32)
        for j in range(nsrc):
            pick = jnp.where(owner_s[j] == b, 1.0, 0.0).astype(F32)
            total = total + nbuf[j * nrows : j * nrows + 2 * NEAR, :].astype(F32) * pick
        fills.append(jnp.concatenate([total[:NEAR] * held, total[NEAR:] * held], axis=1).astype(BF16))
    fill = jnp.concatenate(fills, axis=0)
    for i in range(wparts):
        cuts = [b * nrows + wrow + i * NEAR for b in range(nsrc)]
        left = jnp.concatenate([nbuf[cut : cut + NEAR, :] for cut in cuts], axis=0)
        nacc[i * 128 : (i + 1) * 128, :] = lax.dot_general(
            left, fill, (((0,), (0,)), ((), ())), preferred_element_type=F32
        )
    by_real = nacc[pl.ds(pl.multiple_of(me * outs, outs), outs), :]
    by_imag = nacc[pl.ds(pl.multiple_of(sout + me * outs, outs), outs), :]
    near = jnp.concatenate(
        [by_real[:, :RECV] - by_imag[:, RECV:], by_imag[:, :RECV] + by_real[:, RECV:]], axis=0
    )

    for copy in sent_p:
        copy.wait()
    pred = near + pbuf[0:span, :]
    for j in range(1, nsrc):
        pred = pred + pbuf[j * span : (j + 1) * span, :]
    mine = pl.ds(pl.multiple_of(here * span, span), span)
    gath[mine, :] = pred
    sent_g = exchange("freq", here, freq_peers, lambda peer: gath.at[mine, :], gath, span, gsend, grecv)

    base = here * (wrows - 2 * HALO) - HALO
    local[4].wait()
    local[5].wait()
    first, last = start_s[0], end_s[0]

    def delayed(u, c, n):
        t = base + u
        v = t - (third(n) - LAGS_T // 2)
        valid = (t >= first) & (t < last) & (v >= first) & (v < last) & (n < NU)
        turns = ((F_LOW + (c >> 1)) * v + (NFFT // 4) * (c & 1)) & (NFFT - 1)
        return jnp.where(valid, cosine(turns) * scale, 0.0)

    rows_cn = comps * NP
    shape = (rows_cn, 128)
    row = iota(shape, 0)
    u_t = delayed(iota(shape, 1), row >> 5, row & (NP - 1))
    shape = (wrows, rows_cn)
    lane = iota(shape, 1)
    u_n = delayed(iota(shape, 0), lane >> 5, lane & (NP - 1))

    for copy in sent_g:
        copy.wait()

    size = comps * outs
    whole = gath[...]
    lane = iota((size, RECV), 1)
    shifts[0:size, :] = jnp.where(lane == RECV - 1, 0.0, pltpu.roll(whole, RECV - 1, 1))
    shifts[size : 2 * size, :] = whole
    shifts[2 * size :, :] = jnp.where(lane == 0, 0.0, pltpu.roll(whole, 1, 1))
    waves = jnp.concatenate([shifts[pl.ds(s, k3, stride=outs), :] for s in range(outs)], axis=1)

    parts = split3(waves)
    stacked = jnp.concatenate([*parts, trace], axis=0).astype(BF16)
    waves3 = stacked[: 3 * k3]
    pair = lax.dot_general(waves3, stacked, (((1,), (1,)), ((), ())), preferred_element_type=F32)
    pair = pair[:k3] + pair[k3 : 2 * k3] + pair[2 * k3 :]
    slot = pl.ds(pl.multiple_of(me * k3, k3), k3)
    zused = 3 * k3 + wrows
    zbuf[slot, 0:zused] = pair
    sent_z = exchange("src", me, src_peers, lambda peer: zbuf.at[slot, :], zbuf, k3, zsend, zrecv)

    shape = (rows_cn, 3 * k3)
    row, lane = iota(shape, 0), iota(shape, 1)
    lane = jnp.where(lane >= 2 * k3, lane - 2 * k3, jnp.where(lane >= k3, lane - k3, lane))
    n = row & (NP - 1)
    same = ((lane >> log_c) == n - 3 * third(n)) & ((lane & (comps - 1)) == (row >> 5)) & (n < NU)
    pick_rows = jnp.where(same, 1.0, 0.0).astype(F32)
    shape = (k3, rows_cn)
    row, lane = iota(shape, 0), iota(shape, 1)
    n = lane & (NP - 1)
    same = ((row >> log_c) == n - 3 * third(n)) & ((row & (comps - 1)) == (lane >> 5)) & (n < NU)
    pick_lanes = jnp.where(same, 1.0, 0.0).astype(BF16)

    hbig[...] = hdot(u_t[:, :wrows], u_n)
    for copy in sent_z:
        copy.wait()
    both = zbuf[0:k3, :]
    for j in range(1, nsrc):
        both = both + zbuf[j * k3 : (j + 1) * k3, :]
    corr = both[:, 0:k3] + both[:, k3 : 2 * k3] + both[:, 2 * k3 : 3 * k3]
    cross = both[:, 3 * k3 : zused]

    corr3 = jnp.concatenate(split3(corr), axis=0).astype(BF16)
    cross3 = jnp.concatenate(split3(cross), axis=0).astype(BF16)
    pick_bf = pick_rows.astype(BF16)
    grid = bdot(pick_bf, bdot(corr3, pick_lanes).astype(BF16)) * hbig[...]
    spread = bdot(pick_bf, cross3) * u_t[:, :wrows]
    gram = grid[:NP]
    right = spread[:NP]
    for d in range(1, comps):
        gram = gram + grid[d * NP : (d + 1) * NP]
        right = right + spread[d * NP : (d + 1) * NP]
    tiles = gram[:, :128]
    for d in range(1, rows_cn // 128):
        tiles = tiles + gram[:, d * 128 : (d + 1) * 128]
    tiles = tiles + pltpu.roll(tiles, 64, 1)
    tiles = tiles + pltpu.roll(tiles, 32, 1)
    right = jnp.sum(right, axis=1, keepdims=True)

    damping = float(wrows * total_out * RECV)
    shape = (NP, 128)
    row, lane = iota(shape, 0), iota(shape, 1)
    centre = LAGS_T // 2 * LAGS_X + LAGS_X // 2
    right = right + jnp.where(row == centre, damping, 0.0)
    system = jnp.where(lane == 127, right, tiles + jnp.where(row == lane, damping, 0.0))
    for k in range(0, NU, 3):
        cols = [jnp.broadcast_to(system[:, k + i : k + i + 1], (NP, 128)) for i in range(3)]
        rows = [system[k + i : k + i + 1, :] for i in range(3)]
        inner = [[cols[j][k + i : k + i + 1, :] for j in range(3)] for i in range(3)]
        for i in range(3):
            inverse = 1.0 / inner[i][i]
            rows[i] = rows[i] * inverse
            scaled = [None if j <= i else inner[i][j] * inverse for j in range(3)]
            for j in range(3):
                if j > i:
                    rows[j] = rows[j] - inner[j][i] * rows[i]
                    for m in range(i + 1, 3):
                        inner[j][m] = inner[j][m] - inner[j][i] * scaled[m]
            for m in range(i + 1, 3):
                inner[i][m] = scaled[m]
        rows[1] = rows[1] - inner[1][2] * rows[2]
        rows[0] = rows[0] - inner[0][1] * rows[1] - inner[0][2] * rows[2]
        system = system - (cols[0] * rows[0] + cols[1] * rows[1] + cols[2] * rows[2])
        for i in range(3):
            system = jnp.where(row == k + i, rows[i], system)
    coef = system[:, 127:128]
    across = jnp.sum(jnp.where(row == lane, coef, 0.0), axis=0, keepdims=True)
    filt[...] = across[:, :NU]

    weighted = pick_rows * jnp.concatenate([coef] * comps, axis=0)
    mix = jnp.concatenate(split3(hdot(u_n, weighted)), axis=0).astype(BF16)
    matched = bdot(mix, waves3)
    matched = matched[:wrows] + matched[wrows : 2 * wrows] + matched[2 * wrows :]
    t = base + iota((wrows, 1), 0)
    keep = jnp.where((t >= first) & (t < last), 1.0, 0.0).astype(F32)
    result = (trace - matched) * keep
    for s in range(outs):
        rec32[pl.ds(s, wrows, stride=outs), :] = result[:, s * RECV : (s + 1) * RECV]
    prim[...] = rec32[...].astype(BF16)


def solution(mesh):
    nsrc, nfreq = mesh.shape["src"], mesh.shape["freq"]

    def body(data, recip, gap, owner, weights, start_row, end_row, recorded):
        assert data.shape[1] == 1
        wrows, outs, recv = recorded.shape
        comps = 2 * nfreq
        k3 = LAGS_X * comps
        zlanes = -(-(3 * k3 + wrows) // 128) * 128
        recip, weights, gap = recip.swapaxes(2, 3), weights.swapaxes(2, 3), gap.T
        sout = weights.shape[2]
        anywhere = pl.BlockSpec(memory_space=pl.ANY)
        vmem = pl.BlockSpec(memory_space=pltpu.VMEM)
        dma = pltpu.SemaphoreType.DMA
        primaries, filters = pl.pallas_call(
            functools.partial(kernel, nsrc, nfreq, comps, sout, 1.0 / math.sqrt(nfreq)),
            out_shape=(
                jax.ShapeDtypeStruct((wrows * outs, recv), BF16),
                jax.ShapeDtypeStruct((1, NU), F32),
            ),
            in_specs=[anywhere] * 8,
            out_specs=(vmem, vmem),
            scratch_shapes=[
                pltpu.SMEM(owner.shape, jnp.int32),
                pltpu.SMEM(start_row.shape, jnp.int32),
                pltpu.SMEM(end_row.shape, jnp.int32),
                pltpu.VMEM(data.shape, BF16),
                pltpu.VMEM(weights.shape, BF16),
                pltpu.VMEM(recip.shape, BF16),
                pltpu.VMEM(gap.shape, jnp.int32),
                pltpu.VMEM(recorded.shape, BF16),
                pltpu.VMEM((nsrc * (3 * NEAR + 2 * sout // 128 * NEAR), recv), BF16),
                pltpu.VMEM((2 * sout, 2 * recv), F32),
                pltpu.VMEM((nsrc * 2 * outs, recv), F32),
                pltpu.VMEM((nsrc * 2 * outs, recv), F32),
                pltpu.VMEM((comps * outs, recv), F32),
                pltpu.VMEM((k3 * outs, recv), F32),
                pltpu.VMEM((wrows * outs, recv), F32),
                pltpu.VMEM((nsrc * k3, zlanes), F32),
                pltpu.VMEM((comps * NP, comps * NP), F32),
                dma((6,)),
                dma((2 * CHUNKS,)),
                dma((nsrc,)), dma((nsrc,)),
                dma((nsrc,)), dma((nsrc,)),
                dma((nfreq,)), dma((nfreq,)),
                dma((nsrc,)), dma((nsrc,)),
            ],
            compiler_params=pltpu.CompilerParams(
                collective_id=0, has_side_effects=True, vmem_limit_bytes=56 * 1024 * 1024
            ),
            name="multiples",
        )(data, recip, gap, owner, weights, start_row, end_row, recorded)
        return primaries.reshape(wrows, outs, recv), filters

    placed = (
        P(None, "freq", None, "src"),
        P(None, "freq", None, "src"),
        P(None, "src"),
        P(),
        P(None, "freq", "src", None),
        P("freq"),
        P("freq"),
        P("freq", "src", None),
    )
    return jax.shard_map(
        body,
        mesh=mesh,
        in_specs=placed,
        out_specs=(P("freq", "src", None), P("freq", None)),
        check_vma=False,
    )
```

```python
import functools
import math

import jax
import jax.numpy as jnp
from jax import lax
from jax.experimental import pallas as pl
from jax.experimental.pallas import tpu as pltpu
from jax.sharding import PartitionSpec as P

RECV = 128
NFFT = 512
F_LOW = 40
NEAR = 16
HALO = 8
LAGS_T = 9
LAGS_X = 3
NU = LAGS_T * LAGS_X
NP = 32
CHUNKS = 4
F32 = jnp.float32
BF16 = jnp.bfloat16


def hdot(a, b, dims=((1,), (0,))):
    return lax.dot_general(
        a, b, (dims, ((), ())), precision=lax.Precision.HIGHEST, preferred_element_type=F32
    )


def bdot(a, b):
    return jnp.dot(a, b, preferred_element_type=F32)


def iota(shape, dim):
    return lax.broadcasted_iota(jnp.int32, shape, dim)


def split3(x):
    high = x.astype(BF16).astype(F32)
    rest = x - high
    middle = rest.astype(BF16).astype(F32)
    return high, middle, rest - middle


def cosine(turns):
    y = (turns - NFFT // 2).astype(F32) * (math.pi / NFFT)
    square = y * y
    series = jnp.full_like(y, 1.0 / 6227020800.0)
    for factor in (-1.0 / 39916800.0, 1.0 / 362880.0, -1.0 / 5040.0, 1.0 / 120.0, -1.0 / 6.0, 1.0):
        series = series * square + factor
    sine = series * y
    return 2.0 * sine * sine - 1.0


def third(n):
    return (n * 171) >> 9


def kernel(
    nsrc, nfreq, comps, total_out, scale,
    data, recip, gap, owner, weights, start, end, recorded,
    prim, filt,
    nbuf, nacc, pout, pbuf, gath, shifts, rec32, zbuf, hbig,
    rsend, rrecv, psend, precv, gsend, grecv, zsend, zrecv,
):
    me = lax.axis_index("src")
    here = lax.axis_index("freq")
    depth = data.shape[3]
    wrows = recorded.shape[0]
    outs = recorded.shape[1]
    step = depth // CHUNKS
    sout = total_out
    log_c = comps.bit_length() - 1
    k3 = LAGS_X * comps

    src_peers = [lax.rem(me + k, nsrc) for k in range(1, nsrc)]
    freq_peers = [lax.rem(here + k, nfreq) for k in range(1, nfreq)]
    barrier = pltpu.get_barrier_semaphore()
    for peer in src_peers:
        pl.semaphore_signal(barrier, inc=1, device_id={"src": peer}, device_id_type=pl.DeviceIdType.MESH)
    for peer in freq_peers:
        pl.semaphore_signal(barrier, inc=1, device_id={"freq": peer}, device_id_type=pl.DeviceIdType.MESH)

    def exchange(axis, mine, peers, src_of, buf, rows, send, recv):
        slot = buf.at[pl.ds(pl.multiple_of(mine * rows, rows), rows), :]
        copies = []
        for k, peer in enumerate(peers):
            copies.append(
                pltpu.make_async_remote_copy(
                    src_ref=src_of(peer),
                    dst_ref=slot,
                    send_sem=send.at[k],
                    recv_sem=recv.at[k],
                    device_id={axis: peer},
                    device_id_type=pl.DeviceIdType.MESH,
                )
            )
            copies[-1].start()
        return copies

    wrow = 3 * NEAR
    wparts = 2 * sout // 128
    nrows = wrow + wparts * NEAR
    at = pl.multiple_of(me * nrows, NEAR)
    nbuf[pl.ds(at, 2 * NEAR), :] = recip[...].reshape(2 * NEAR, RECV)
    gap_t = jnp.where(gap[...] == 1, 1.0, 0.0).astype(F32)
    nbuf[pl.ds(at + 2 * NEAR, NEAR), :] = gap_t.astype(BF16)
    present = 1.0 - gap_t.T
    near_w = weights[:, 0, :, :NEAR].reshape(2 * sout, NEAR).astype(F32)
    for i in range(wparts):
        nbuf[pl.ds(at + wrow + i * NEAR, NEAR), :] = near_w[i * 128 : (i + 1) * 128].T.astype(BF16)
    pl.semaphore_wait(barrier, nsrc - 1 + nfreq - 1)
    own = nbuf.at[pl.ds(at, nrows), :]
    sent_r = exchange("src", me, src_peers, lambda peer: own, nbuf, nrows, rsend, rrecv)

    lane = iota((RECV, 128), 1)
    kept = jnp.concatenate([present] * (128 // NEAR), axis=1)
    heads = [
        jnp.where((lane < NEAR) & (kept < 0.5), 0.0, data[ci, 0, :, :128].astype(F32)).astype(BF16)
        for ci in range(2)
    ]
    heads = jnp.concatenate(heads, axis=0)
    acc = jnp.zeros((2 * sout, 2 * RECV), F32)
    for i in range(CHUNKS):
        cut = slice(i * step, (i + 1) * step)
        left = weights[:, 0, :, cut].reshape(2 * sout, step)
        right = data[:, 0, :, cut].reshape(2 * RECV, step)
        if i == 0:
            right = jnp.concatenate([heads, right[:, 128:]], axis=1)
        acc = acc + lax.dot_general(left, right, (((1,), (1,)), ((), ())), preferred_element_type=F32)
    real = acc[:sout, :RECV] - acc[sout:, RECV:]
    imag = acc[sout:, :RECV] + acc[:sout, RECV:]

    span = 2 * outs
    for d in range(nsrc):
        pout[d * span : d * span + outs, :] = real[d * outs : (d + 1) * outs]
        pout[d * span + outs : (d + 1) * span, :] = imag[d * outs : (d + 1) * outs]

    def block_for(peer):
        return pout.at[pl.ds(pl.multiple_of(peer * span, span), span), :]

    sent_p = exchange("src", me, src_peers, block_for, pbuf, span, psend, precv)
    mine = pl.ds(pl.multiple_of(me * span, span), span)
    pbuf[mine, :] = pout[mine, :]

    rec32[...] = recorded[...].astype(F32).reshape(wrows * outs, RECV)
    trace = jnp.concatenate([rec32[pl.ds(s, wrows, stride=outs), :] for s in range(outs)], axis=1)

    for copy in sent_r:
        copy.wait_recv()
    fills = []
    for b in range(nsrc):
        held = nbuf[b * nrows + 2 * NEAR : b * nrows + 3 * NEAR, :].astype(F32)
        total = jnp.zeros((2 * NEAR, RECV), F32)
        for j in range(nsrc):
            pick = jnp.where(owner[j] == b, 1.0, 0.0).astype(F32)
            total = total + nbuf[j * nrows : j * nrows + 2 * NEAR, :].astype(F32) * pick
        fills.append(jnp.concatenate([total[:NEAR] * held, total[NEAR:] * held], axis=1).astype(BF16))
    fill = jnp.concatenate(fills, axis=0)
    for i in range(wparts):
        cuts = [b * nrows + wrow + i * NEAR for b in range(nsrc)]
        left = jnp.concatenate([nbuf[cut : cut + NEAR, :] for cut in cuts], axis=0)
        nacc[i * 128 : (i + 1) * 128, :] = lax.dot_general(
            left, fill, (((0,), (0,)), ((), ())), preferred_element_type=F32
        )
    by_real = nacc[pl.ds(pl.multiple_of(me * outs, outs), outs), :]
    by_imag = nacc[pl.ds(pl.multiple_of(sout + me * outs, outs), outs), :]
    near = jnp.concatenate(
        [by_real[:, :RECV] - by_imag[:, RECV:], by_imag[:, :RECV] + by_real[:, RECV:]], axis=0
    )

    for copy in sent_p:
        copy.wait_recv()
    pred = near + pbuf[0:span, :]
    for j in range(1, nsrc):
        pred = pred + pbuf[j * span : (j + 1) * span, :]
    mine = pl.ds(pl.multiple_of(here * span, span), span)
    gath[mine, :] = pred
    sent_g = exchange("freq", here, freq_peers, lambda peer: gath.at[mine, :], gath, span, gsend, grecv)

    base = here * (wrows - 2 * HALO) - HALO
    first, last = start[0], end[0]

    def delayed(u, c, n):
        t = base + u
        v = t - (third(n) - LAGS_T // 2)
        valid = (t >= first) & (t < last) & (v >= first) & (v < last) & (n < NU)
        turns = ((F_LOW + (c >> 1)) * v + (NFFT // 4) * (c & 1)) & (NFFT - 1)
        return jnp.where(valid, cosine(turns) * scale, 0.0)

    rows_cn = comps * NP
    shape = (rows_cn, 128)
    row = iota(shape, 0)
    u_t = delayed(iota(shape, 1), row >> 5, row & (NP - 1))
    shape = (wrows, rows_cn)
    lane = iota(shape, 1)
    u_n = delayed(iota(shape, 0), lane >> 5, lane & (NP - 1))

    for copy in sent_g:
        copy.wait_recv()

    size = comps * outs
    whole = gath[...]
    lane = iota((size, RECV), 1)
    shifts[0:size, :] = jnp.where(lane == RECV - 1, 0.0, pltpu.roll(whole, RECV - 1, 1))
    shifts[size : 2 * size, :] = whole
    shifts[2 * size :, :] = jnp.where(lane == 0, 0.0, pltpu.roll(whole, 1, 1))
    waves = jnp.concatenate([shifts[pl.ds(s, k3, stride=outs), :] for s in range(outs)], axis=1)

    parts = split3(waves)
    stacked = jnp.concatenate([*parts, trace], axis=0).astype(BF16)
    waves3 = stacked[: 3 * k3]
    pair = lax.dot_general(waves3, stacked, (((1,), (1,)), ((), ())), preferred_element_type=F32)
    pair = pair[:k3] + pair[k3 : 2 * k3] + pair[2 * k3 :]
    slot = pl.ds(pl.multiple_of(me * k3, k3), k3)
    zused = 3 * k3 + wrows
    zbuf[slot, 0:zused] = pair
    sent_z = exchange("src", me, src_peers, lambda peer: zbuf.at[slot, :], zbuf, k3, zsend, zrecv)

    shape = (rows_cn, 3 * k3)
    row, lane = iota(shape, 0), iota(shape, 1)
    lane = jnp.where(lane >= 2 * k3, lane - 2 * k3, jnp.where(lane >= k3, lane - k3, lane))
    n = row & (NP - 1)
    same = ((lane >> log_c) == n - 3 * third(n)) & ((lane & (comps - 1)) == (row >> 5)) & (n < NU)
    pick_rows = jnp.where(same, 1.0, 0.0).astype(F32)
    shape = (k3, rows_cn)
    row, lane = iota(shape, 0), iota(shape, 1)
    n = lane & (NP - 1)
    same = ((row >> log_c) == n - 3 * third(n)) & ((row & (comps - 1)) == (lane >> 5)) & (n < NU)
    pick_lanes = jnp.where(same, 1.0, 0.0).astype(BF16)

    u_parts = jnp.concatenate(split3(u_n), axis=0).astype(BF16)
    hbig[...] = hdot(u_t[:, :wrows], u_n)
    for copy in sent_z:
        copy.wait_recv()
    both = zbuf[0:k3, :]
    for j in range(1, nsrc):
        both = both + zbuf[j * k3 : (j + 1) * k3, :]
    corr = both[:, 0:k3] + both[:, k3 : 2 * k3] + both[:, 2 * k3 : 3 * k3]
    cross = both[:, 3 * k3 : zused]

    corr3 = jnp.concatenate(split3(corr), axis=0).astype(BF16)
    cross3 = jnp.concatenate(split3(cross), axis=0).astype(BF16)
    pick_bf = pick_rows.astype(BF16)
    grid = bdot(pick_bf, bdot(corr3, pick_lanes).astype(BF16)) * hbig[...]
    spread = bdot(pick_bf, cross3) * u_t[:, :wrows]
    gram = grid[:NP]
    right = spread[:NP]
    for d in range(1, comps):
        gram = gram + grid[d * NP : (d + 1) * NP]
        right = right + spread[d * NP : (d + 1) * NP]
    tiles = gram[:, :128]
    for d in range(1, rows_cn // 128):
        tiles = tiles + gram[:, d * 128 : (d + 1) * 128]
    tiles = tiles + pltpu.roll(tiles, 64, 1)
    tiles = tiles + pltpu.roll(tiles, 32, 1)
    right = jnp.sum(right, axis=1, keepdims=True)

    damping = float(wrows * total_out * RECV)
    shape = (NP, 128)
    row, lane = iota(shape, 0), iota(shape, 1)
    centre = LAGS_T // 2 * LAGS_X + LAGS_X // 2
    right = right + jnp.where(row == centre, damping, 0.0)
    system = jnp.where(lane == 127, right, tiles + jnp.where(row == lane, damping, 0.0))
    for k in range(0, NU, 3):
        cols = [jnp.broadcast_to(system[:, k + i : k + i + 1], (NP, 128)) for i in range(3)]
        rows = [system[k + i : k + i + 1, :] for i in range(3)]
        inner = [[cols[j][k + i : k + i + 1, :] for j in range(3)] for i in range(3)]
        for i in range(3):
            inverse = 1.0 / inner[i][i]
            rows[i] = rows[i] * inverse
            scaled = [None if j <= i else inner[i][j] * inverse for j in range(3)]
            for j in range(3):
                if j > i:
                    rows[j] = rows[j] - inner[j][i] * rows[i]
                    for m in range(i + 1, 3):
                        inner[j][m] = inner[j][m] - inner[j][i] * scaled[m]
            for m in range(i + 1, 3):
                inner[i][m] = scaled[m]
        rows[1] = rows[1] - inner[1][2] * rows[2]
        rows[0] = rows[0] - inner[0][1] * rows[1] - inner[0][2] * rows[2]
        system = system - (cols[0] * rows[0] + cols[1] * rows[1] + cols[2] * rows[2])
        for i in range(3):
            system = jnp.where(row == k + i, rows[i], system)
    coef = system[:, 127:128]
    across = jnp.sum(jnp.where(row == lane, coef, 0.0), axis=0, keepdims=True)
    filt[...] = across[:, :NU]

    mix = jnp.zeros((3 * wrows, 3 * k3), F32)
    for part in split3(coef):
        weighted = pick_rows * jnp.concatenate([part] * comps, axis=0)
        mix = mix + bdot(u_parts, weighted.astype(BF16))
    mix = mix[:wrows] + mix[wrows : 2 * wrows] + mix[2 * wrows :]
    mix = jnp.concatenate(split3(mix), axis=0).astype(BF16)
    matched = bdot(mix, waves3)
    matched = matched[:wrows] + matched[wrows : 2 * wrows] + matched[2 * wrows :]
    t = base + iota((wrows, 1), 0)
    keep = jnp.where((t >= first) & (t < last), 1.0, 0.0).astype(F32)
    result = (trace - matched) * keep
    for s in range(outs):
        rec32[pl.ds(s, wrows, stride=outs), :] = result[:, s * RECV : (s + 1) * RECV]
    prim[...] = rec32[...].astype(BF16)
    for copy in sent_r + sent_p + sent_g + sent_z:
        copy.wait_send()


def finish(prim, filt, prim_out, filt_out):
    prim_out[...] = prim[...]
    filt_out[...] = filt[...]


def solution(mesh):
    nsrc, nfreq = mesh.shape["src"], mesh.shape["freq"]

    def body(data, recip, gap, owner, weights, start_row, end_row, recorded):
        assert data.shape[1] == 1
        wrows, outs, recv = recorded.shape
        comps = 2 * nfreq
        k3 = LAGS_X * comps
        zlanes = -(-(3 * k3 + wrows) // 128) * 128
        recip, weights, gap = recip.swapaxes(2, 3), weights.swapaxes(2, 3), gap.T
        sout = weights.shape[2]
        scalar = pl.BlockSpec(memory_space=pltpu.SMEM)
        limit = 16 * 1024 * 1024 + 8 * 4 * (comps * NP) ** 2
        vmem = pl.BlockSpec(memory_space=pltpu.VMEM)
        dma = pltpu.SemaphoreType.DMA
        primaries, filters = pl.pallas_call(
            functools.partial(kernel, nsrc, nfreq, comps, sout, 1.0 / math.sqrt(nfreq)),
            out_shape=(
                jax.ShapeDtypeStruct((wrows * outs, recv), BF16),
                jax.ShapeDtypeStruct((1, NU), F32),
            ),
            in_specs=[vmem, vmem, vmem, scalar, vmem, scalar, scalar, vmem],
            out_specs=(vmem, vmem),
            scratch_shapes=[
                pltpu.VMEM((nsrc * (3 * NEAR + 2 * sout // 128 * NEAR), recv), BF16),
                pltpu.VMEM((2 * sout, 2 * recv), F32),
                pltpu.VMEM((nsrc * 2 * outs, recv), F32),
                pltpu.VMEM((nsrc * 2 * outs, recv), F32),
                pltpu.VMEM((comps * outs, recv), F32),
                pltpu.VMEM((k3 * outs, recv), F32),
                pltpu.VMEM((wrows * outs, recv), F32),
                pltpu.VMEM((nsrc * k3, zlanes), F32),
                pltpu.VMEM((comps * NP, comps * NP), F32),
                dma((nsrc,)), dma((nsrc,)),
                dma((nsrc,)), dma((nsrc,)),
                dma((nfreq,)), dma((nfreq,)),
                dma((nsrc,)), dma((nsrc,)),
            ],
            compiler_params=pltpu.CompilerParams(
                collective_id=0, has_side_effects=True, vmem_limit_bytes=limit
            ),
            name="multiples",
        )(data, recip, gap, owner, weights, start_row, end_row, recorded)
        return tuple(
            pl.pallas_call(
                finish,
                out_shape=(
                    jax.ShapeDtypeStruct((wrows, outs, recv), BF16),
                    jax.ShapeDtypeStruct((1, NU), F32),
                ),
                in_specs=[vmem] * 2,
                out_specs=(vmem, vmem),
                name="finish",
            )(primaries.reshape(wrows, outs, recv), filters)
        )

    placed = (
        P(None, "freq", None, "src"),
        P(None, "freq", None, "src"),
        P(None, "src"),
        P(),
        P(None, "freq", "src", None),
        P("freq"),
        P("freq"),
        P("freq", "src", None),
    )
    return jax.shard_map(
        body,
        mesh=mesh,
        in_specs=placed,
        out_specs=(P("freq", "src", None), P("freq", None)),
        check_vma=False,
    )
```

```python
import functools
import math

import jax
import jax.numpy as jnp
from jax import lax
from jax.experimental import pallas as pl
from jax.experimental.pallas import tpu as pltpu
from jax.sharding import PartitionSpec as P

RECV = 128
NFFT = 512
F_LOW = 40
NEAR = 16
HALO = 8
LAGS_T = 9
LAGS_X = 3
NU = LAGS_T * LAGS_X
NP = 32
CHUNKS = 4
F32 = jnp.float32
BF16 = jnp.bfloat16


def hdot(a, b, dims=((1,), (0,))):
    return lax.dot_general(
        a, b, (dims, ((), ())), precision=lax.Precision.HIGHEST, preferred_element_type=F32
    )


def bdot(a, b):
    return jnp.dot(a, b, preferred_element_type=F32)


def iota(shape, dim):
    return lax.broadcasted_iota(jnp.int32, shape, dim)


def split3(x):
    high = x.astype(BF16).astype(F32)
    rest = x - high
    middle = rest.astype(BF16).astype(F32)
    return high, middle, rest - middle


def cosine(turns):
    y = (turns - NFFT // 2).astype(F32) * (math.pi / NFFT)
    square = y * y
    series = jnp.full_like(y, 1.0 / 6227020800.0)
    for factor in (-1.0 / 39916800.0, 1.0 / 362880.0, -1.0 / 5040.0, 1.0 / 120.0, -1.0 / 6.0, 1.0):
        series = series * square + factor
    sine = series * y
    return 2.0 * sine * sine - 1.0


def third(n):
    return (n * 171) >> 9


def kernel(
    nsrc, nfreq, comps, total_out, scale,
    data, recip, gap, owner, weights, start, end, recorded,
    prim, filt,
    owner_s, start_s, end_s, dbuf, wbuf, rin, gin, recb, nbuf, nacc, pout, pbuf, gath, shifts, rec32, zbuf, hbig,
    lsem, dsem, rsend, rrecv, psend, precv, gsend, grecv, zsend, zrecv,
):
    me = lax.axis_index("src")
    here = lax.axis_index("freq")
    depth = data.shape[3]
    wrows = recorded.shape[0]
    outs = recorded.shape[1]
    step = depth // CHUNKS
    sout = total_out
    log_c = comps.bit_length() - 1
    k3 = LAGS_X * comps

    local = [
        pltpu.make_async_copy(recip, rin, lsem.at[0]),
        pltpu.make_async_copy(gap, gin, lsem.at[1]),
        pltpu.make_async_copy(recorded, recb, lsem.at[2]),
        pltpu.make_async_copy(owner, owner_s, lsem.at[3]),
        pltpu.make_async_copy(start, start_s, lsem.at[4]),
        pltpu.make_async_copy(end, end_s, lsem.at[5]),
    ]
    for copy in local:
        copy.start()
    big = []
    for i in range(CHUNKS):
        cut = pl.ds(i * step, step)
        big.append(
            (
                pltpu.make_async_copy(data.at[:, :, :, cut], dbuf.at[:, :, :, cut], dsem.at[2 * i]),
                pltpu.make_async_copy(weights.at[:, :, :, cut], wbuf.at[:, :, :, cut], dsem.at[2 * i + 1]),
            )
        )
        for copy in big[-1]:
            copy.start()

    src_peers = [lax.rem(me + k, nsrc) for k in range(1, nsrc)]
    freq_peers = [lax.rem(here + k, nfreq) for k in range(1, nfreq)]
    barrier = pltpu.get_barrier_semaphore()
    for peer in src_peers:
        pl.semaphore_signal(barrier, inc=1, device_id={"src": peer}, device_id_type=pl.DeviceIdType.MESH)
    for peer in freq_peers:
        pl.semaphore_signal(barrier, inc=1, device_id={"freq": peer}, device_id_type=pl.DeviceIdType.MESH)

    def exchange(axis, mine, peers, src_of, buf, rows, send, recv):
        slot = buf.at[pl.ds(pl.multiple_of(mine * rows, rows), rows), :]
        copies = []
        for k, peer in enumerate(peers):
            copies.append(
                pltpu.make_async_remote_copy(
                    src_ref=src_of(peer),
                    dst_ref=slot,
                    send_sem=send.at[k],
                    recv_sem=recv.at[k],
                    device_id={axis: peer},
                    device_id_type=pl.DeviceIdType.MESH,
                )
            )
            copies[-1].start()
        return copies

    wrow = 3 * NEAR
    wparts = 2 * sout // 128
    nrows = wrow + wparts * NEAR
    at = pl.multiple_of(me * nrows, NEAR)
    local[0].wait()
    nbuf[pl.ds(at, 2 * NEAR), :] = rin[...].reshape(2 * NEAR, RECV)
    local[1].wait()
    gap_t = jnp.where(gin[...] == 1, 1.0, 0.0).astype(F32)
    nbuf[pl.ds(at + 2 * NEAR, NEAR), :] = gap_t.astype(BF16)
    present = 1.0 - gap_t.T
    for copy in big[0]:
        copy.wait()
    near_w = wbuf[:, 0, :, :NEAR].reshape(2 * sout, NEAR).astype(F32)
    for i in range(wparts):
        nbuf[pl.ds(at + wrow + i * NEAR, NEAR), :] = near_w[i * 128 : (i + 1) * 128].T.astype(BF16)
    pl.semaphore_wait(barrier, nsrc - 1 + nfreq - 1)
    own = nbuf.at[pl.ds(at, nrows), :]
    sent_r = exchange("src", me, src_peers, lambda peer: own, nbuf, nrows, rsend, rrecv)

    acc = jnp.zeros((2 * RECV, 2 * sout), F32)
    for i in range(CHUNKS):
        if i == 0:
            for ci in range(2):
                head = dbuf[ci, 0, :, :NEAR].astype(F32)
                dbuf[ci, 0, :, :NEAR] = jnp.where(present > 0.5, head, 0.0).astype(BF16)
        else:
            for copy in big[i]:
                copy.wait()
        cut = slice(i * step, (i + 1) * step)
        left = wbuf[:, 0, :, cut].reshape(2 * sout, step)
        right = dbuf[:, 0, :, cut].reshape(2 * RECV, step)
        acc = acc + lax.dot_general(right, left, (((1,), (1,)), ((), ())), preferred_element_type=F32)
    acc = acc.T
    real = acc[:sout, :RECV] - acc[sout:, RECV:]
    imag = acc[sout:, :RECV] + acc[:sout, RECV:]

    span = 2 * outs
    for d in range(nsrc):
        pout[d * span : d * span + outs, :] = real[d * outs : (d + 1) * outs]
        pout[d * span + outs : (d + 1) * span, :] = imag[d * outs : (d + 1) * outs]

    def block_for(peer):
        return pout.at[pl.ds(pl.multiple_of(peer * span, span), span), :]

    sent_p = exchange("src", me, src_peers, block_for, pbuf, span, psend, precv)
    mine = pl.ds(pl.multiple_of(me * span, span), span)
    pbuf[mine, :] = pout[mine, :]

    local[2].wait()
    rec32[...] = recb[...].astype(F32).reshape(wrows * outs, RECV)
    trace = jnp.concatenate([rec32[pl.ds(s, wrows, stride=outs), :] for s in range(outs)], axis=1)

    for copy in sent_r:
        copy.wait_recv()
    local[3].wait()
    fills = []
    for b in range(nsrc):
        held = nbuf[b * nrows + 2 * NEAR : b * nrows + 3 * NEAR, :].astype(F32)
        total = jnp.zeros((2 * NEAR, RECV), F32)
        for j in range(nsrc):
            pick = jnp.where(owner_s[j] == b, 1.0, 0.0).astype(F32)
            total = total + nbuf[j * nrows : j * nrows + 2 * NEAR, :].astype(F32) * pick
        fills.append(jnp.concatenate([total[:NEAR] * held, total[NEAR:] * held], axis=1).astype(BF16))
    fill = jnp.concatenate(fills, axis=0)
    for i in range(wparts):
        cuts = [b * nrows + wrow + i * NEAR for b in range(nsrc)]
        left = jnp.concatenate([nbuf[cut : cut + NEAR, :] for cut in cuts], axis=0)
        nacc[i * 128 : (i + 1) * 128, :] = lax.dot_general(
            left, fill, (((0,), (0,)), ((), ())), preferred_element_type=F32
        )
    by_real = nacc[pl.ds(pl.multiple_of(me * outs, outs), outs), :]
    by_imag = nacc[pl.ds(pl.multiple_of(sout + me * outs, outs), outs), :]
    near = jnp.concatenate(
        [by_real[:, :RECV] - by_imag[:, RECV:], by_imag[:, :RECV] + by_real[:, RECV:]], axis=0
    )

    for copy in sent_p:
        copy.wait_recv()
    pred = near + pbuf[0:span, :]
    for j in range(1, nsrc):
        pred = pred + pbuf[j * span : (j + 1) * span, :]
    mine = pl.ds(pl.multiple_of(here * span, span), span)
    gath[mine, :] = pred
    sent_g = exchange("freq", here, freq_peers, lambda peer: gath.at[mine, :], gath, span, gsend, grecv)

    base = here * (wrows - 2 * HALO) - HALO
    local[4].wait()
    local[5].wait()
    first, last = start_s[0], end_s[0]

    def delayed(u, c, n):
        t = base + u
        v = t - (third(n) - LAGS_T // 2)
        valid = (t >= first) & (t < last) & (v >= first) & (v < last) & (n < NU)
        turns = ((F_LOW + (c >> 1)) * v + (NFFT // 4) * (c & 1)) & (NFFT - 1)
        return jnp.where(valid, cosine(turns) * scale, 0.0)

    rows_cn = comps * NP
    shape = (rows_cn, 128)
    row = iota(shape, 0)
    u_t = delayed(iota(shape, 1), row >> 5, row & (NP - 1))
    shape = (wrows, rows_cn)
    lane = iota(shape, 1)
    u_n = delayed(iota(shape, 0), lane >> 5, lane & (NP - 1))

    for copy in sent_g:
        copy.wait_recv()

    size = comps * outs
    whole = gath[...]
    lane = iota((size, RECV), 1)
    shifts[0:size, :] = jnp.where(lane == RECV - 1, 0.0, pltpu.roll(whole, RECV - 1, 1))
    shifts[size : 2 * size, :] = whole
    shifts[2 * size :, :] = jnp.where(lane == 0, 0.0, pltpu.roll(whole, 1, 1))
    waves = jnp.concatenate([shifts[pl.ds(s, k3, stride=outs), :] for s in range(outs)], axis=1)

    parts = split3(waves)
    stacked = jnp.concatenate([*parts, trace], axis=0).astype(BF16)
    waves3 = stacked[: 3 * k3]
    pair = lax.dot_general(waves3, stacked, (((1,), (1,)), ((), ())), preferred_element_type=F32)
    pair = pair[:k3] + pair[k3 : 2 * k3] + pair[2 * k3 :]
    slot = pl.ds(pl.multiple_of(me * k3, k3), k3)
    zused = 3 * k3 + wrows
    zbuf[slot, 0:zused] = pair
    sent_z = exchange("src", me, src_peers, lambda peer: zbuf.at[slot, :], zbuf, k3, zsend, zrecv)

    shape = (rows_cn, 3 * k3)
    row, lane = iota(shape, 0), iota(shape, 1)
    lane = jnp.where(lane >= 2 * k3, lane - 2 * k3, jnp.where(lane >= k3, lane - k3, lane))
    n = row & (NP - 1)
    same = ((lane >> log_c) == n - 3 * third(n)) & ((lane & (comps - 1)) == (row >> 5)) & (n < NU)
    pick_rows = jnp.where(same, 1.0, 0.0).astype(F32)
    shape = (k3, rows_cn)
    row, lane = iota(shape, 0), iota(shape, 1)
    n = lane & (NP - 1)
    same = ((row >> log_c) == n - 3 * third(n)) & ((row & (comps - 1)) == (lane >> 5)) & (n < NU)
    pick_lanes = jnp.where(same, 1.0, 0.0).astype(BF16)

    u_parts = jnp.concatenate(split3(u_n), axis=0).astype(BF16)
    hbig[...] = hdot(u_t[:, :wrows], u_n)
    for copy in sent_z:
        copy.wait_recv()
    both = zbuf[0:k3, :]
    for j in range(1, nsrc):
        both = both + zbuf[j * k3 : (j + 1) * k3, :]
    corr = both[:, 0:k3] + both[:, k3 : 2 * k3] + both[:, 2 * k3 : 3 * k3]
    cross = both[:, 3 * k3 : zused]

    corr3 = jnp.concatenate(split3(corr), axis=0).astype(BF16)
    cross3 = jnp.concatenate(split3(cross), axis=0).astype(BF16)
    pick_bf = pick_rows.astype(BF16)
    grid = bdot(pick_bf, bdot(corr3, pick_lanes).astype(BF16)) * hbig[...]
    spread = bdot(pick_bf, cross3) * u_t[:, :wrows]
    gram = grid[:NP]
    right = spread[:NP]
    for d in range(1, comps):
        gram = gram + grid[d * NP : (d + 1) * NP]
        right = right + spread[d * NP : (d + 1) * NP]
    tiles = gram[:, :128]
    for d in range(1, rows_cn // 128):
        tiles = tiles + gram[:, d * 128 : (d + 1) * 128]
    tiles = tiles + pltpu.roll(tiles, 64, 1)
    tiles = tiles + pltpu.roll(tiles, 32, 1)
    right = jnp.sum(right, axis=1, keepdims=True)

    damping = float(wrows * total_out * RECV)
    shape = (NP, 128)
    row, lane = iota(shape, 0), iota(shape, 1)
    centre = LAGS_T // 2 * LAGS_X + LAGS_X // 2
    right = right + jnp.where(row == centre, damping, 0.0)
    system = jnp.where(lane == 127, right, tiles + jnp.where(row == lane, damping, 0.0))
    for k in range(0, NU, 3):
        cols = [jnp.broadcast_to(system[:, k + i : k + i + 1], (NP, 128)) for i in range(3)]
        rows = [system[k + i : k + i + 1, :] for i in range(3)]
        inner = [[cols[j][k + i : k + i + 1, :] for j in range(3)] for i in range(3)]
        for i in range(3):
            inverse = 1.0 / inner[i][i]
            rows[i] = rows[i] * inverse
            scaled = [None if j <= i else inner[i][j] * inverse for j in range(3)]
            for j in range(3):
                if j > i:
                    rows[j] = rows[j] - inner[j][i] * rows[i]
                    for m in range(i + 1, 3):
                        inner[j][m] = inner[j][m] - inner[j][i] * scaled[m]
            for m in range(i + 1, 3):
                inner[i][m] = scaled[m]
        rows[1] = rows[1] - inner[1][2] * rows[2]
        rows[0] = rows[0] - inner[0][1] * rows[1] - inner[0][2] * rows[2]
        system = system - (cols[0] * rows[0] + cols[1] * rows[1] + cols[2] * rows[2])
        for i in range(3):
            system = jnp.where(row == k + i, rows[i], system)
    coef = system[:, 127:128]
    across = jnp.sum(jnp.where(row == lane, coef, 0.0), axis=0, keepdims=True)
    filt[...] = across[:, :NU]

    mix = jnp.zeros((3 * wrows, 3 * k3), F32)
    for part in split3(coef):
        weighted = pick_rows * jnp.concatenate([part] * comps, axis=0)
        mix = mix + bdot(u_parts, weighted.astype(BF16))
    mix = mix[:wrows] + mix[wrows : 2 * wrows] + mix[2 * wrows :]
    mix = jnp.concatenate(split3(mix), axis=0).astype(BF16)
    matched = bdot(mix, waves3)
    matched = matched[:wrows] + matched[wrows : 2 * wrows] + matched[2 * wrows :]
    t = base + iota((wrows, 1), 0)
    keep = jnp.where((t >= first) & (t < last), 1.0, 0.0).astype(F32)
    result = (trace - matched) * keep
    for s in range(outs):
        rec32[pl.ds(s, wrows, stride=outs), :] = result[:, s * RECV : (s + 1) * RECV]
    prim[...] = rec32[...].astype(BF16)
    for copy in sent_r + sent_p + sent_g + sent_z:
        copy.wait_send()


def finish(prim, filt, prim_out, filt_out):
    prim_out[...] = prim[...]
    filt_out[...] = filt[...]


def solution(mesh):
    nsrc, nfreq = mesh.shape["src"], mesh.shape["freq"]

    def body(data, recip, gap, owner, weights, start_row, end_row, recorded):
        assert data.shape[1] == 1
        wrows, outs, recv = recorded.shape
        comps = 2 * nfreq
        k3 = LAGS_X * comps
        zlanes = -(-(3 * k3 + wrows) // 128) * 128
        recip, weights, gap = recip.swapaxes(2, 3), weights.swapaxes(2, 3), gap.T
        sout = weights.shape[2]
        anywhere = pl.BlockSpec(memory_space=pl.ANY)
        vmem = pl.BlockSpec(memory_space=pltpu.VMEM)
        dma = pltpu.SemaphoreType.DMA
        primaries, filters = pl.pallas_call(
            functools.partial(kernel, nsrc, nfreq, comps, sout, 1.0 / math.sqrt(nfreq)),
            out_shape=(
                jax.ShapeDtypeStruct((wrows * outs, recv), BF16),
                jax.ShapeDtypeStruct((1, NU), F32),
            ),
            in_specs=[anywhere] * 8,
            out_specs=(vmem, vmem),
            scratch_shapes=[
                pltpu.SMEM(owner.shape, jnp.int32),
                pltpu.SMEM(start_row.shape, jnp.int32),
                pltpu.SMEM(end_row.shape, jnp.int32),
                pltpu.VMEM(data.shape, BF16),
                pltpu.VMEM(weights.shape, BF16),
                pltpu.VMEM(recip.shape, BF16),
                pltpu.VMEM(gap.shape, jnp.int32),
                pltpu.VMEM(recorded.shape, BF16),
                pltpu.VMEM((nsrc * (3 * NEAR + 2 * sout // 128 * NEAR), recv), BF16),
                pltpu.VMEM((2 * sout, 2 * recv), F32),
                pltpu.VMEM((nsrc * 2 * outs, recv), F32),
                pltpu.VMEM((nsrc * 2 * outs, recv), F32),
                pltpu.VMEM((comps * outs, recv), F32),
                pltpu.VMEM((k3 * outs, recv), F32),
                pltpu.VMEM((wrows * outs, recv), F32),
                pltpu.VMEM((nsrc * k3, zlanes), F32),
                pltpu.VMEM((comps * NP, comps * NP), F32),
                dma((6,)),
                dma((2 * CHUNKS,)),
                dma((nsrc,)), dma((nsrc,)),
                dma((nsrc,)), dma((nsrc,)),
                dma((nfreq,)), dma((nfreq,)),
                dma((nsrc,)), dma((nsrc,)),
            ],
            compiler_params=pltpu.CompilerParams(
                collective_id=0, has_side_effects=True, vmem_limit_bytes=56 * 1024 * 1024
            ),
            name="multiples",
        )(data, recip, gap, owner, weights, start_row, end_row, recorded)
        return tuple(
            pl.pallas_call(
                finish,
                out_shape=(
                    jax.ShapeDtypeStruct((wrows, outs, recv), BF16),
                    jax.ShapeDtypeStruct((1, NU), F32),
                ),
                in_specs=[vmem] * 2,
                out_specs=(vmem, vmem),
                compiler_params=pltpu.CompilerParams(vmem_limit_bytes=56 * 1024 * 1024),
                name="finish",
            )(primaries.reshape(wrows, outs, recv), filters)
        )

    placed = (
        P(None, "freq", None, "src"),
        P(None, "freq", None, "src"),
        P(None, "src"),
        P(),
        P(None, "freq", "src", None),
        P("freq"),
        P("freq"),
        P("freq", "src", None),
    )
    return jax.shard_map(
        body,
        mesh=mesh,
        in_specs=placed,
        out_specs=(P("freq", "src", None), P("freq", None)),
        check_vma=False,
    )
```

```python
import functools
import math

import jax
import jax.numpy as jnp
from jax import lax
from jax.experimental import pallas as pl
from jax.experimental.pallas import tpu as pltpu
from jax.sharding import PartitionSpec as P

RECV = 128
NFFT = 512
F_LOW = 40
NEAR = 16
HALO = 8
LAGS_T = 9
LAGS_X = 3
NU = LAGS_T * LAGS_X
NP = 32
CHUNKS = 4
F32 = jnp.float32
BF16 = jnp.bfloat16


def hdot(a, b, dims=((1,), (0,))):
    return lax.dot_general(
        a, b, (dims, ((), ())), precision=lax.Precision.HIGHEST, preferred_element_type=F32
    )


def bdot(a, b):
    return jnp.dot(a, b, preferred_element_type=F32)


def iota(shape, dim):
    return lax.broadcasted_iota(jnp.int32, shape, dim)


def split3(x):
    high = x.astype(BF16).astype(F32)
    rest = x - high
    middle = rest.astype(BF16).astype(F32)
    return high, middle, rest - middle


def cosine(turns):
    y = (turns - NFFT // 2).astype(F32) * (math.pi / NFFT)
    square = y * y
    series = jnp.full_like(y, 1.0 / 6227020800.0)
    for factor in (-1.0 / 39916800.0, 1.0 / 362880.0, -1.0 / 5040.0, 1.0 / 120.0, -1.0 / 6.0, 1.0):
        series = series * square + factor
    sine = series * y
    return 2.0 * sine * sine - 1.0


def third(n):
    return (n * 171) >> 9


def partners(index, count):
    if count & (count - 1):
        return [lax.rem(index + k, count) for k in range(1, count)]
    found = []
    for flips in range(count - 1, 0, -1):
        peer = 0
        for bit in range(count.bit_length() - 1):
            value = 1 << bit
            peer = peer + lax.rem(lax.div(index, value) + (flips >> bit) % 2, 2) * value
        found.append(peer)
    return found


def inverse_of(x):
    guess = pl.reciprocal(x, approx=True)
    return guess * (2.0 - x * guess)


def kernel(
    nsrc, nfreq, comps, total_out, scale,
    data, recip, gap, owner, weights, start, end, recorded,
    prim, filt,
    owner_s, start_s, end_s, dbuf, wbuf, rin, gin, recb, nbuf, nacc, pout, pbuf, gath, shifts, rec32, zbuf, hbig,
    lsem, dsem, rsend, rrecv, psend, precv, gsend, grecv, zsend, zrecv,
):
    me = lax.axis_index("src")
    here = lax.axis_index("freq")
    depth = data.shape[3]
    wrows = recorded.shape[0]
    outs = recorded.shape[1]
    step = depth // CHUNKS
    sout = total_out
    log_c = comps.bit_length() - 1
    k3 = LAGS_X * comps

    local = [
        pltpu.make_async_copy(recip, rin, lsem.at[0]),
        pltpu.make_async_copy(gap, gin, lsem.at[1]),
        pltpu.make_async_copy(recorded, recb, lsem.at[2]),
        pltpu.make_async_copy(owner, owner_s, lsem.at[3]),
        pltpu.make_async_copy(start, start_s, lsem.at[4]),
        pltpu.make_async_copy(end, end_s, lsem.at[5]),
    ]
    for copy in local:
        copy.start()
    big = []
    for i in range(CHUNKS):
        cut = pl.ds(i * step, step)
        big.append(
            (
                pltpu.make_async_copy(data.at[:, :, :, cut], dbuf.at[:, :, :, cut], dsem.at[2 * i]),
                pltpu.make_async_copy(weights.at[:, :, :, cut], wbuf.at[:, :, :, cut], dsem.at[2 * i + 1]),
            )
        )
        for copy in big[-1]:
            copy.start()

    src_peers = partners(me, nsrc)
    freq_peers = partners(here, nfreq)
    barrier = pltpu.get_barrier_semaphore()
    for peer in src_peers:
        pl.semaphore_signal(barrier, inc=1, device_id={"src": peer}, device_id_type=pl.DeviceIdType.MESH)
    for peer in freq_peers:
        pl.semaphore_signal(barrier, inc=1, device_id={"freq": peer}, device_id_type=pl.DeviceIdType.MESH)

    def exchange(axis, mine, peers, src_of, buf, rows, send, recv):
        slot = buf.at[pl.ds(pl.multiple_of(mine * rows, rows), rows), :]
        copies = []
        for k, peer in enumerate(peers):
            copies.append(
                pltpu.make_async_remote_copy(
                    src_ref=src_of(peer),
                    dst_ref=slot,
                    send_sem=send.at[k],
                    recv_sem=recv.at[k],
                    device_id={axis: peer},
                    device_id_type=pl.DeviceIdType.MESH,
                )
            )
            copies[-1].start()
        return copies

    wrow = 3 * NEAR
    wparts = 2 * sout // 128
    nrows = wrow + wparts * NEAR
    at = pl.multiple_of(me * nrows, NEAR)
    local[0].wait()
    nbuf[pl.ds(at, 2 * NEAR), :] = rin[...].reshape(2 * NEAR, RECV)
    local[1].wait()
    gap_t = jnp.where(gin[...] == 1, 1.0, 0.0).astype(F32)
    nbuf[pl.ds(at + 2 * NEAR, NEAR), :] = gap_t.astype(BF16)
    present = 1.0 - gap_t.T
    for copy in big[0]:
        copy.wait()
    near_w = wbuf[:, 0, :, :NEAR].reshape(2 * sout, NEAR).astype(F32)
    for i in range(wparts):
        nbuf[pl.ds(at + wrow + i * NEAR, NEAR), :] = near_w[i * 128 : (i + 1) * 128].T.astype(BF16)
    pl.semaphore_wait(barrier, nsrc - 1 + nfreq - 1)
    own = nbuf.at[pl.ds(at, nrows), :]
    sent_r = exchange("src", me, src_peers, lambda peer: own, nbuf, nrows, rsend, rrecv)

    acc = jnp.zeros((2 * RECV, 2 * sout), F32)
    for i in range(CHUNKS):
        if i == 0:
            for ci in range(2):
                head = dbuf[ci, 0, :, :NEAR].astype(F32)
                dbuf[ci, 0, :, :NEAR] = jnp.where(present > 0.5, head, 0.0).astype(BF16)
        else:
            for copy in big[i]:
                copy.wait()
        cut = slice(i * step, (i + 1) * step)
        left = wbuf[:, 0, :, cut].reshape(2 * sout, step)
        right = dbuf[:, 0, :, cut].reshape(2 * RECV, step)
        acc = acc + lax.dot_general(right, left, (((1,), (1,)), ((), ())), preferred_element_type=F32)
    acc = acc.T
    real = acc[:sout, :RECV] - acc[sout:, RECV:]
    imag = acc[sout:, :RECV] + acc[:sout, RECV:]

    span = 2 * outs
    for d in range(nsrc):
        pout[d * span : d * span + outs, :] = real[d * outs : (d + 1) * outs]
        pout[d * span + outs : (d + 1) * span, :] = imag[d * outs : (d + 1) * outs]

    def block_for(peer):
        return pout.at[pl.ds(pl.multiple_of(peer * span, span), span), :]

    sent_p = exchange("src", me, src_peers, block_for, pbuf, span, psend, precv)
    mine = pl.ds(pl.multiple_of(me * span, span), span)
    pbuf[mine, :] = pout[mine, :]

    local[2].wait()
    rec32[...] = recb[...].astype(F32).reshape(wrows * outs, RECV)
    trace = jnp.concatenate([rec32[pl.ds(s, wrows, stride=outs), :] for s in range(outs)], axis=1)

    for copy in sent_r:
        copy.wait_recv()
    local[3].wait()
    fills = []
    for b in range(nsrc):
        held = nbuf[b * nrows + 2 * NEAR : b * nrows + 3 * NEAR, :].astype(F32)
        total = jnp.zeros((2 * NEAR, RECV), F32)
        for j in range(nsrc):
            pick = jnp.where(owner_s[j] == b, 1.0, 0.0).astype(F32)
            total = total + nbuf[j * nrows : j * nrows + 2 * NEAR, :].astype(F32) * pick
        fills.append(jnp.concatenate([total[:NEAR] * held, total[NEAR:] * held], axis=1).astype(BF16))
    fill = jnp.concatenate(fills, axis=0)
    for i in range(wparts):
        cuts = [b * nrows + wrow + i * NEAR for b in range(nsrc)]
        left = jnp.concatenate([nbuf[cut : cut + NEAR, :] for cut in cuts], axis=0)
        nacc[i * 128 : (i + 1) * 128, :] = lax.dot_general(
            left, fill, (((0,), (0,)), ((), ())), preferred_element_type=F32
        )
    by_real = nacc[pl.ds(pl.multiple_of(me * outs, outs), outs), :]
    by_imag = nacc[pl.ds(pl.multiple_of(sout + me * outs, outs), outs), :]
    near = jnp.concatenate(
        [by_real[:, :RECV] - by_imag[:, RECV:], by_imag[:, :RECV] + by_real[:, RECV:]], axis=0
    )

    for copy in sent_p:
        copy.wait_recv()
    pred = near + pbuf[0:span, :]
    for j in range(1, nsrc):
        pred = pred + pbuf[j * span : (j + 1) * span, :]
    mine = pl.ds(pl.multiple_of(here * span, span), span)
    gath[mine, :] = pred
    sent_g = exchange("freq", here, freq_peers, lambda peer: gath.at[mine, :], gath, span, gsend, grecv)

    base = here * (wrows - 2 * HALO) - HALO
    local[4].wait()
    local[5].wait()
    first, last = start_s[0], end_s[0]

    def delayed(u, c, n):
        t = base + u
        v = t - (third(n) - LAGS_T // 2)
        valid = (t >= first) & (t < last) & (v >= first) & (v < last) & (n < NU)
        turns = ((F_LOW + (c >> 1)) * v + (NFFT // 4) * (c & 1)) & (NFFT - 1)
        return jnp.where(valid, cosine(turns) * scale, 0.0)

    rows_cn = comps * NP
    shape = (rows_cn, 128)
    row = iota(shape, 0)
    u_t = delayed(iota(shape, 1), row >> 5, row & (NP - 1))
    shape = (wrows, rows_cn)
    lane = iota(shape, 1)
    u_n = delayed(iota(shape, 0), lane >> 5, lane & (NP - 1))

    for copy in sent_g:
        copy.wait_recv()

    size = comps * outs
    whole = gath[...]
    lane = iota((size, RECV), 1)
    shifts[0:size, :] = jnp.where(lane == RECV - 1, 0.0, pltpu.roll(whole, RECV - 1, 1))
    shifts[size : 2 * size, :] = whole
    shifts[2 * size :, :] = jnp.where(lane == 0, 0.0, pltpu.roll(whole, 1, 1))
    waves = jnp.concatenate([shifts[pl.ds(s, k3, stride=outs), :] for s in range(outs)], axis=1)

    parts = split3(waves)
    stacked = jnp.concatenate([*parts, trace], axis=0).astype(BF16)
    waves3 = stacked[: 3 * k3]
    pair = lax.dot_general(waves3, stacked, (((1,), (1,)), ((), ())), preferred_element_type=F32)
    pair = pair[:k3] + pair[k3 : 2 * k3] + pair[2 * k3 :]
    slot = pl.ds(pl.multiple_of(me * k3, k3), k3)
    zused = 3 * k3 + wrows
    zbuf[slot, 0:zused] = pair
    sent_z = exchange("src", me, src_peers, lambda peer: zbuf.at[slot, :], zbuf, k3, zsend, zrecv)

    shape = (rows_cn, 3 * k3)
    row, lane = iota(shape, 0), iota(shape, 1)
    lane = jnp.where(lane >= 2 * k3, lane - 2 * k3, jnp.where(lane >= k3, lane - k3, lane))
    n = row & (NP - 1)
    same = ((lane >> log_c) == n - 3 * third(n)) & ((lane & (comps - 1)) == (row >> 5)) & (n < NU)
    pick_rows = jnp.where(same, 1.0, 0.0).astype(F32)
    shape = (k3, rows_cn)
    row, lane = iota(shape, 0), iota(shape, 1)
    n = lane & (NP - 1)
    same = ((row >> log_c) == n - 3 * third(n)) & ((row & (comps - 1)) == (lane >> 5)) & (n < NU)
    pick_lanes = jnp.where(same, 1.0, 0.0).astype(BF16)

    u_parts = jnp.concatenate(split3(u_n), axis=0).astype(BF16)
    hbig[...] = hdot(u_t[:, :wrows], u_n)
    for copy in sent_z:
        copy.wait_recv()
    both = zbuf[0:k3, :]
    for j in range(1, nsrc):
        both = both + zbuf[j * k3 : (j + 1) * k3, :]
    corr = both[:, 0:k3] + both[:, k3 : 2 * k3] + both[:, 2 * k3 : 3 * k3]
    cross = both[:, 3 * k3 : zused]

    corr3 = jnp.concatenate(split3(corr), axis=0).astype(BF16)
    cross3 = jnp.concatenate(split3(cross), axis=0).astype(BF16)
    pick_bf = pick_rows.astype(BF16)
    grid = bdot(pick_bf, bdot(corr3, pick_lanes).astype(BF16)) * hbig[...]
    spread = bdot(pick_bf, cross3) * u_t[:, :wrows]
    gram = grid[:NP]
    right = spread[:NP]
    for d in range(1, comps):
        gram = gram + grid[d * NP : (d + 1) * NP]
        right = right + spread[d * NP : (d + 1) * NP]
    tiles = gram[:, :128]
    for d in range(1, rows_cn // 128):
        tiles = tiles + gram[:, d * 128 : (d + 1) * 128]
    tiles = tiles + pltpu.roll(tiles, 64, 1)
    tiles = tiles + pltpu.roll(tiles, 32, 1)
    right = jnp.sum(right, axis=1, keepdims=True)

    damping = float(wrows * total_out * RECV)
    shape = (NP, 128)
    row, lane = iota(shape, 0), iota(shape, 1)
    centre = LAGS_T // 2 * LAGS_X + LAGS_X // 2
    right = right + jnp.where(row == centre, damping, 0.0)
    system = jnp.where(lane == 127, right, tiles + jnp.where(row == lane, damping, 0.0))
    for k in range(0, NU, 3):
        cols = [jnp.broadcast_to(system[:, k + i : k + i + 1], (NP, 128)) for i in range(3)]
        rows = [system[k + i : k + i + 1, :] for i in range(3)]
        inner = [[cols[j][k + i : k + i + 1, :] for j in range(3)] for i in range(3)]
        for i in range(3):
            inverse = inverse_of(inner[i][i])
            rows[i] = rows[i] * inverse
            scaled = [None if j <= i else inner[i][j] * inverse for j in range(3)]
            for j in range(3):
                if j > i:
                    rows[j] = rows[j] - inner[j][i] * rows[i]
                    for m in range(i + 1, 3):
                        inner[j][m] = inner[j][m] - inner[j][i] * scaled[m]
            for m in range(i + 1, 3):
                inner[i][m] = scaled[m]
        rows[1] = rows[1] - inner[1][2] * rows[2]
        rows[0] = rows[0] - inner[0][1] * rows[1] - inner[0][2] * rows[2]
        system = system - (cols[0] * rows[0] + cols[1] * rows[1] + cols[2] * rows[2])
        for i in range(3):
            system = jnp.where(row == k + i, rows[i], system)
    coef = system[:, 127:128]
    across = jnp.sum(jnp.where(row == lane, coef, 0.0), axis=0, keepdims=True)
    filt[...] = across[:, :NU]

    mix = jnp.zeros((3 * wrows, 3 * k3), F32)
    for part in split3(coef):
        weighted = pick_rows * jnp.concatenate([part] * comps, axis=0)
        mix = mix + bdot(u_parts, weighted.astype(BF16))
    mix = mix[:wrows] + mix[wrows : 2 * wrows] + mix[2 * wrows :]
    mix = jnp.concatenate(split3(mix), axis=0).astype(BF16)
    matched = bdot(mix, waves3)
    matched = matched[:wrows] + matched[wrows : 2 * wrows] + matched[2 * wrows :]
    t = base + iota((wrows, 1), 0)
    keep = jnp.where((t >= first) & (t < last), 1.0, 0.0).astype(F32)
    result = (trace - matched) * keep
    for s in range(outs):
        rec32[pl.ds(s, wrows, stride=outs), :] = result[:, s * RECV : (s + 1) * RECV]
    prim[...] = rec32[...].astype(BF16)
    for copy in sent_r + sent_p + sent_g + sent_z:
        copy.wait_send()


def finish(prim, filt, prim_out, filt_out):
    prim_out[...] = prim[...]
    filt_out[...] = filt[...]


def solution(mesh):
    nsrc, nfreq = mesh.shape["src"], mesh.shape["freq"]

    def body(data, recip, gap, owner, weights, start_row, end_row, recorded):
        assert data.shape[1] == 1
        wrows, outs, recv = recorded.shape
        comps = 2 * nfreq
        k3 = LAGS_X * comps
        zlanes = -(-(3 * k3 + wrows) // 128) * 128
        recip, weights, gap = recip.swapaxes(2, 3), weights.swapaxes(2, 3), gap.T
        sout = weights.shape[2]
        anywhere = pl.BlockSpec(memory_space=pl.ANY)
        vmem = pl.BlockSpec(memory_space=pltpu.VMEM)
        dma = pltpu.SemaphoreType.DMA
        primaries, filters = pl.pallas_call(
            functools.partial(kernel, nsrc, nfreq, comps, sout, 1.0 / math.sqrt(nfreq)),
            out_shape=(
                jax.ShapeDtypeStruct((wrows * outs, recv), BF16),
                jax.ShapeDtypeStruct((1, NU), F32),
            ),
            in_specs=[anywhere] * 8,
            out_specs=(vmem, vmem),
            scratch_shapes=[
                pltpu.SMEM(owner.shape, jnp.int32),
                pltpu.SMEM(start_row.shape, jnp.int32),
                pltpu.SMEM(end_row.shape, jnp.int32),
                pltpu.VMEM(data.shape, BF16),
                pltpu.VMEM(weights.shape, BF16),
                pltpu.VMEM(recip.shape, BF16),
                pltpu.VMEM(gap.shape, jnp.int32),
                pltpu.VMEM(recorded.shape, BF16),
                pltpu.VMEM((nsrc * (3 * NEAR + 2 * sout // 128 * NEAR), recv), BF16),
                pltpu.VMEM((2 * sout, 2 * recv), F32),
                pltpu.VMEM((nsrc * 2 * outs, recv), F32),
                pltpu.VMEM((nsrc * 2 * outs, recv), F32),
                pltpu.VMEM((comps * outs, recv), F32),
                pltpu.VMEM((k3 * outs, recv), F32),
                pltpu.VMEM((wrows * outs, recv), F32),
                pltpu.VMEM((nsrc * k3, zlanes), F32),
                pltpu.VMEM((comps * NP, comps * NP), F32),
                dma((6,)),
                dma((2 * CHUNKS,)),
                dma((nsrc,)), dma((nsrc,)),
                dma((nsrc,)), dma((nsrc,)),
                dma((nfreq,)), dma((nfreq,)),
                dma((nsrc,)), dma((nsrc,)),
            ],
            compiler_params=pltpu.CompilerParams(
                collective_id=0, has_side_effects=True, vmem_limit_bytes=56 * 1024 * 1024
            ),
            name="multiples",
        )(data, recip, gap, owner, weights, start_row, end_row, recorded)
        return tuple(
            pl.pallas_call(
                finish,
                out_shape=(
                    jax.ShapeDtypeStruct((wrows, outs, recv), BF16),
                    jax.ShapeDtypeStruct((1, NU), F32),
                ),
                in_specs=[vmem] * 2,
                out_specs=(vmem, vmem),
                compiler_params=pltpu.CompilerParams(vmem_limit_bytes=56 * 1024 * 1024),
                name="finish",
            )(primaries.reshape(wrows, outs, recv), filters)
        )

    placed = (
        P(None, "freq", None, "src"),
        P(None, "freq", None, "src"),
        P(None, "src"),
        P(),
        P(None, "freq", "src", None),
        P("freq"),
        P("freq"),
        P("freq", "src", None),
    )
    return jax.shard_map(
        body,
        mesh=mesh,
        in_specs=placed,
        out_specs=(P("freq", "src", None), P("freq", None)),
        check_vma=False,
    )
```

```python
import functools
import math

import jax
import jax.numpy as jnp
from jax import lax
from jax.experimental import pallas as pl
from jax.experimental.pallas import tpu as pltpu
from jax.sharding import PartitionSpec as P

RECV = 128
NFFT = 512
F_LOW = 40
NEAR = 16
HALO = 8
LAGS_T = 9
LAGS_X = 3
NU = LAGS_T * LAGS_X
NP = 32
CHUNKS = 4
F32 = jnp.float32
BF16 = jnp.bfloat16


def hdot(a, b, dims=((1,), (0,))):
    return lax.dot_general(
        a, b, (dims, ((), ())), precision=lax.Precision.HIGHEST, preferred_element_type=F32
    )


def bdot(a, b):
    return jnp.dot(a, b, preferred_element_type=F32)


def iota(shape, dim):
    return lax.broadcasted_iota(jnp.int32, shape, dim)


def split3(x):
    high = x.astype(BF16).astype(F32)
    rest = x - high
    middle = rest.astype(BF16).astype(F32)
    return high, middle, rest - middle


def cosine(turns):
    y = (turns - NFFT // 2).astype(F32) * (math.pi / NFFT)
    square = y * y
    series = jnp.full_like(y, 1.0 / 6227020800.0)
    for factor in (-1.0 / 39916800.0, 1.0 / 362880.0, -1.0 / 5040.0, 1.0 / 120.0, -1.0 / 6.0, 1.0):
        series = series * square + factor
    sine = series * y
    return 2.0 * sine * sine - 1.0


def third(n):
    return (n * 171) >> 9


def inverse_of(x):
    guess = pl.reciprocal(x, approx=True)
    return guess * (2.0 - x * guess)


def kernel(
    nsrc, nfreq, comps, total_out, scale,
    data, recip, gap, owner, weights, start, end, recorded,
    prim, filt,
    owner_s, start_s, end_s, dbuf, wbuf, rin, gin, recb, nbuf, nacc, pout, pbuf, gath, shifts, rec32, zbuf, hbig,
    lsem, dsem, rsend, rrecv, psend, precv, gsend, grecv, zsend, zrecv,
):
    me = lax.axis_index("src")
    here = lax.axis_index("freq")
    depth = data.shape[3]
    wrows = recorded.shape[0]
    outs = recorded.shape[1]
    step = depth // CHUNKS
    sout = total_out
    log_c = comps.bit_length() - 1
    k3 = LAGS_X * comps

    local = [
        pltpu.make_async_copy(recip, rin, lsem.at[0]),
        pltpu.make_async_copy(gap, gin, lsem.at[1]),
        pltpu.make_async_copy(recorded, recb, lsem.at[2]),
        pltpu.make_async_copy(owner, owner_s, lsem.at[3]),
        pltpu.make_async_copy(start, start_s, lsem.at[4]),
        pltpu.make_async_copy(end, end_s, lsem.at[5]),
    ]
    for copy in local:
        copy.start()
    big = []
    for i in range(CHUNKS):
        cut = pl.ds(i * step, step)
        big.append(
            (
                pltpu.make_async_copy(data.at[:, :, :, cut], dbuf.at[:, :, :, cut], dsem.at[2 * i]),
                pltpu.make_async_copy(weights.at[:, :, :, cut], wbuf.at[:, :, :, cut], dsem.at[2 * i + 1]),
            )
        )
        for copy in big[-1]:
            copy.start()

    src_peers = [lax.rem(me + k, nsrc) for k in range(1, nsrc)]
    freq_peers = [lax.rem(here + k, nfreq) for k in range(1, nfreq)]
    barrier = pltpu.get_barrier_semaphore()
    for peer in src_peers:
        pl.semaphore_signal(barrier, inc=1, device_id={"src": peer}, device_id_type=pl.DeviceIdType.MESH)
    for peer in freq_peers:
        pl.semaphore_signal(barrier, inc=1, device_id={"freq": peer}, device_id_type=pl.DeviceIdType.MESH)

    def exchange(axis, mine, peers, src_of, buf, rows, send, recv):
        slot = buf.at[pl.ds(pl.multiple_of(mine * rows, rows), rows), :]
        copies = []
        for k, peer in enumerate(peers):
            copies.append(
                pltpu.make_async_remote_copy(
                    src_ref=src_of(peer),
                    dst_ref=slot,
                    send_sem=send.at[k],
                    recv_sem=recv.at[k],
                    device_id={axis: peer},
                    device_id_type=pl.DeviceIdType.MESH,
                )
            )
            copies[-1].start()
        return copies

    wrow = 3 * NEAR
    wparts = 2 * sout // 128
    nrows = wrow + wparts * NEAR
    at = pl.multiple_of(me * nrows, NEAR)
    local[0].wait()
    nbuf[pl.ds(at, 2 * NEAR), :] = rin[...].reshape(2 * NEAR, RECV)
    local[1].wait()
    gap_t = jnp.where(gin[...] == 1, 1.0, 0.0).astype(F32)
    nbuf[pl.ds(at + 2 * NEAR, NEAR), :] = gap_t.astype(BF16)
    present = 1.0 - gap_t.T
    for copy in big[0]:
        copy.wait()
    near_w = wbuf[:, 0, :, :NEAR].reshape(2 * sout, NEAR).astype(F32)
    for i in range(wparts):
        nbuf[pl.ds(at + wrow + i * NEAR, NEAR), :] = near_w[i * 128 : (i + 1) * 128].T.astype(BF16)
    pl.semaphore_wait(barrier, nsrc - 1 + nfreq - 1)
    own = nbuf.at[pl.ds(at, nrows), :]
    sent_r = exchange("src", me, src_peers, lambda peer: own, nbuf, nrows, rsend, rrecv)

    acc = jnp.zeros((2 * RECV, 2 * sout), F32)
    for i in range(CHUNKS):
        if i == 0:
            for ci in range(2):
                head = dbuf[ci, 0, :, :NEAR].astype(F32)
                dbuf[ci, 0, :, :NEAR] = jnp.where(present > 0.5, head, 0.0).astype(BF16)
        else:
            for copy in big[i]:
                copy.wait()
        cut = slice(i * step, (i + 1) * step)
        left = wbuf[:, 0, :, cut].reshape(2 * sout, step)
        right = dbuf[:, 0, :, cut].reshape(2 * RECV, step)
        acc = acc + lax.dot_general(right, left, (((1,), (1,)), ((), ())), preferred_element_type=F32)
    acc = acc.T
    real = acc[:sout, :RECV] - acc[sout:, RECV:]
    imag = acc[sout:, :RECV] + acc[:sout, RECV:]

    span = 2 * outs
    for d in range(nsrc):
        pout[d * span : d * span + outs, :] = real[d * outs : (d + 1) * outs]
        pout[d * span + outs : (d + 1) * span, :] = imag[d * outs : (d + 1) * outs]

    def block_for(peer):
        return pout.at[pl.ds(pl.multiple_of(peer * span, span), span), :]

    sent_p = exchange("src", me, src_peers, block_for, pbuf, span, psend, precv)
    mine = pl.ds(pl.multiple_of(me * span, span), span)
    pbuf[mine, :] = pout[mine, :]

    local[2].wait()
    rec32[...] = recb[...].astype(F32).reshape(wrows * outs, RECV)
    trace = jnp.concatenate([rec32[pl.ds(s, wrows, stride=outs), :] for s in range(outs)], axis=1)

    for copy in sent_r:
        copy.wait_recv()
    local[3].wait()
    fills = []
    for b in range(nsrc):
        held = nbuf[b * nrows + 2 * NEAR : b * nrows + 3 * NEAR, :].astype(F32)
        total = jnp.zeros((2 * NEAR, RECV), F32)
        for j in range(nsrc):
            pick = jnp.where(owner_s[j] == b, 1.0, 0.0).astype(F32)
            total = total + nbuf[j * nrows : j * nrows + 2 * NEAR, :].astype(F32) * pick
        fills.append(jnp.concatenate([total[:NEAR] * held, total[NEAR:] * held], axis=1).astype(BF16))
    fill = jnp.concatenate(fills, axis=0)
    for i in range(wparts):
        cuts = [b * nrows + wrow + i * NEAR for b in range(nsrc)]
        left = jnp.concatenate([nbuf[cut : cut + NEAR, :] for cut in cuts], axis=0)
        nacc[i * 128 : (i + 1) * 128, :] = lax.dot_general(
            left, fill, (((0,), (0,)), ((), ())), preferred_element_type=F32
        )
    by_real = nacc[pl.ds(pl.multiple_of(me * outs, outs), outs), :]
    by_imag = nacc[pl.ds(pl.multiple_of(sout + me * outs, outs), outs), :]
    near = jnp.concatenate(
        [by_real[:, :RECV] - by_imag[:, RECV:], by_imag[:, :RECV] + by_real[:, RECV:]], axis=0
    )

    for copy in sent_p:
        copy.wait_recv()
    pred = near + pbuf[0:span, :]
    for j in range(1, nsrc):
        pred = pred + pbuf[j * span : (j + 1) * span, :]
    mine = pl.ds(pl.multiple_of(here * span, span), span)
    gath[mine, :] = pred
    sent_g = exchange("freq", here, freq_peers, lambda peer: gath.at[mine, :], gath, span, gsend, grecv)

    base = here * (wrows - 2 * HALO) - HALO
    local[4].wait()
    local[5].wait()
    first, last = start_s[0], end_s[0]

    def delayed(u, c, n):
        t = base + u
        v = t - (third(n) - LAGS_T // 2)
        valid = (t >= first) & (t < last) & (v >= first) & (v < last) & (n < NU)
        turns = ((F_LOW + (c >> 1)) * v + (NFFT // 4) * (c & 1)) & (NFFT - 1)
        return jnp.where(valid, cosine(turns) * scale, 0.0)

    rows_cn = comps * NP
    shape = (rows_cn, 128)
    row = iota(shape, 0)
    u_t = delayed(iota(shape, 1), row >> 5, row & (NP - 1))
    shape = (wrows, rows_cn)
    lane = iota(shape, 1)
    u_n = delayed(iota(shape, 0), lane >> 5, lane & (NP - 1))

    for copy in sent_g:
        copy.wait_recv()

    size = comps * outs
    whole = gath[...]
    lane = iota((size, RECV), 1)
    shifts[0:size, :] = jnp.where(lane == RECV - 1, 0.0, pltpu.roll(whole, RECV - 1, 1))
    shifts[size : 2 * size, :] = whole
    shifts[2 * size :, :] = jnp.where(lane == 0, 0.0, pltpu.roll(whole, 1, 1))
    waves = jnp.concatenate([shifts[pl.ds(s, k3, stride=outs), :] for s in range(outs)], axis=1)

    parts = split3(waves)
    stacked = jnp.concatenate([*parts, trace], axis=0).astype(BF16)
    waves3 = stacked[: 3 * k3]
    pair = lax.dot_general(waves3, stacked, (((1,), (1,)), ((), ())), preferred_element_type=F32)
    pair = pair[:k3] + pair[k3 : 2 * k3] + pair[2 * k3 :]
    slot = pl.ds(pl.multiple_of(me * k3, k3), k3)
    zused = 3 * k3 + wrows
    zbuf[slot, 0:zused] = pair
    sent_z = exchange("src", me, src_peers, lambda peer: zbuf.at[slot, :], zbuf, k3, zsend, zrecv)

    shape = (rows_cn, 3 * k3)
    row, lane = iota(shape, 0), iota(shape, 1)
    lane = jnp.where(lane >= 2 * k3, lane - 2 * k3, jnp.where(lane >= k3, lane - k3, lane))
    n = row & (NP - 1)
    same = ((lane >> log_c) == n - 3 * third(n)) & ((lane & (comps - 1)) == (row >> 5)) & (n < NU)
    pick_rows = jnp.where(same, 1.0, 0.0).astype(F32)
    shape = (k3, rows_cn)
    row, lane = iota(shape, 0), iota(shape, 1)
    n = lane & (NP - 1)
    same = ((row >> log_c) == n - 3 * third(n)) & ((row & (comps - 1)) == (lane >> 5)) & (n < NU)
    pick_lanes = jnp.where(same, 1.0, 0.0).astype(BF16)

    u_parts = jnp.concatenate(split3(u_n), axis=0).astype(BF16)
    hbig[...] = hdot(u_t[:, :wrows], u_n)
    for copy in sent_z:
        copy.wait_recv()
    both = zbuf[0:k3, :]
    for j in range(1, nsrc):
        both = both + zbuf[j * k3 : (j + 1) * k3, :]
    corr = both[:, 0:k3] + both[:, k3 : 2 * k3] + both[:, 2 * k3 : 3 * k3]
    cross = both[:, 3 * k3 : zused]

    corr3 = jnp.concatenate(split3(corr), axis=0).astype(BF16)
    cross3 = jnp.concatenate(split3(cross), axis=0).astype(BF16)
    pick_bf = pick_rows.astype(BF16)
    grid = bdot(pick_bf, bdot(corr3, pick_lanes).astype(BF16)) * hbig[...]
    spread = bdot(pick_bf, cross3) * u_t[:, :wrows]
    gram = grid[:NP]
    right = spread[:NP]
    for d in range(1, comps):
        gram = gram + grid[d * NP : (d + 1) * NP]
        right = right + spread[d * NP : (d + 1) * NP]
    tiles = gram[:, :128]
    for d in range(1, rows_cn // 128):
        tiles = tiles + gram[:, d * 128 : (d + 1) * 128]
    tiles = tiles + pltpu.roll(tiles, 64, 1)
    tiles = tiles + pltpu.roll(tiles, 32, 1)
    right = jnp.sum(right, axis=1, keepdims=True)

    damping = float(wrows * total_out * RECV)
    shape = (NP, 128)
    row, lane = iota(shape, 0), iota(shape, 1)
    centre = LAGS_T // 2 * LAGS_X + LAGS_X // 2
    right = right + jnp.where(row == centre, damping, 0.0)
    system = jnp.where(lane == 127, right, tiles + jnp.where(row == lane, damping, 0.0))
    for k in range(0, NU, 3):
        cols = [jnp.broadcast_to(system[:, k + i : k + i + 1], (NP, 128)) for i in range(3)]
        rows = [system[k + i : k + i + 1, :] for i in range(3)]
        inner = [[cols[j][k + i : k + i + 1, :] for j in range(3)] for i in range(3)]
        for i in range(3):
            inverse = inverse_of(inner[i][i])
            rows[i] = rows[i] * inverse
            scaled = [None if j <= i else inner[i][j] * inverse for j in range(3)]
            for j in range(3):
                if j > i:
                    rows[j] = rows[j] - inner[j][i] * rows[i]
                    for m in range(i + 1, 3):
                        inner[j][m] = inner[j][m] - inner[j][i] * scaled[m]
            for m in range(i + 1, 3):
                inner[i][m] = scaled[m]
        rows[1] = rows[1] - inner[1][2] * rows[2]
        rows[0] = rows[0] - inner[0][1] * rows[1] - inner[0][2] * rows[2]
        system = system - (cols[0] * rows[0] + cols[1] * rows[1] + cols[2] * rows[2])
        for i in range(3):
            system = jnp.where(row == k + i, rows[i], system)
    coef = system[:, 127:128]
    across = jnp.sum(jnp.where(row == lane, coef, 0.0), axis=0, keepdims=True)
    filt[...] = across[:, :NU]

    mix = jnp.zeros((3 * wrows, 3 * k3), F32)
    for part in split3(coef):
        weighted = pick_rows * jnp.concatenate([part] * comps, axis=0)
        mix = mix + bdot(u_parts, weighted.astype(BF16))
    mix = mix[:wrows] + mix[wrows : 2 * wrows] + mix[2 * wrows :]
    mix = jnp.concatenate(split3(mix), axis=0).astype(BF16)
    matched = bdot(mix, waves3)
    matched = matched[:wrows] + matched[wrows : 2 * wrows] + matched[2 * wrows :]
    t = base + iota((wrows, 1), 0)
    keep = jnp.where((t >= first) & (t < last), 1.0, 0.0).astype(F32)
    result = (trace - matched) * keep
    for s in range(outs):
        rec32[pl.ds(s, wrows, stride=outs), :] = result[:, s * RECV : (s + 1) * RECV]
    prim[...] = rec32[...].astype(BF16)
    for copy in sent_r + sent_p + sent_g + sent_z:
        copy.wait_send()


def finish(prim, filt, prim_out, filt_out):
    prim_out[...] = prim[...]
    filt_out[...] = filt[...]


def solution(mesh):
    nsrc, nfreq = mesh.shape["src"], mesh.shape["freq"]

    def body(data, recip, gap, owner, weights, start_row, end_row, recorded):
        assert data.shape[1] == 1
        wrows, outs, recv = recorded.shape
        comps = 2 * nfreq
        k3 = LAGS_X * comps
        zlanes = -(-(3 * k3 + wrows) // 128) * 128
        recip, weights, gap = recip.swapaxes(2, 3), weights.swapaxes(2, 3), gap.T
        sout = weights.shape[2]
        anywhere = pl.BlockSpec(memory_space=pl.ANY)
        vmem = pl.BlockSpec(memory_space=pltpu.VMEM)
        dma = pltpu.SemaphoreType.DMA
        primaries, filters = pl.pallas_call(
            functools.partial(kernel, nsrc, nfreq, comps, sout, 1.0 / math.sqrt(nfreq)),
            out_shape=(
                jax.ShapeDtypeStruct((wrows * outs, recv), BF16),
                jax.ShapeDtypeStruct((1, NU), F32),
            ),
            in_specs=[anywhere] * 8,
            out_specs=(vmem, vmem),
            scratch_shapes=[
                pltpu.SMEM(owner.shape, jnp.int32),
                pltpu.SMEM(start_row.shape, jnp.int32),
                pltpu.SMEM(end_row.shape, jnp.int32),
                pltpu.VMEM(data.shape, BF16),
                pltpu.VMEM(weights.shape, BF16),
                pltpu.VMEM(recip.shape, BF16),
                pltpu.VMEM(gap.shape, jnp.int32),
                pltpu.VMEM(recorded.shape, BF16),
                pltpu.VMEM((nsrc * (3 * NEAR + 2 * sout // 128 * NEAR), recv), BF16),
                pltpu.VMEM((2 * sout, 2 * recv), F32),
                pltpu.VMEM((nsrc * 2 * outs, recv), F32),
                pltpu.VMEM((nsrc * 2 * outs, recv), F32),
                pltpu.VMEM((comps * outs, recv), F32),
                pltpu.VMEM((k3 * outs, recv), F32),
                pltpu.VMEM((wrows * outs, recv), F32),
                pltpu.VMEM((nsrc * k3, zlanes), F32),
                pltpu.VMEM((comps * NP, comps * NP), F32),
                dma((6,)),
                dma((2 * CHUNKS,)),
                dma((nsrc,)), dma((nsrc,)),
                dma((nsrc,)), dma((nsrc,)),
                dma((nfreq,)), dma((nfreq,)),
                dma((nsrc,)), dma((nsrc,)),
            ],
            compiler_params=pltpu.CompilerParams(
                collective_id=0, has_side_effects=True, vmem_limit_bytes=56 * 1024 * 1024
            ),
            name="multiples",
        )(data, recip, gap, owner, weights, start_row, end_row, recorded)
        return tuple(
            pl.pallas_call(
                finish,
                out_shape=(
                    jax.ShapeDtypeStruct((wrows, outs, recv), BF16),
                    jax.ShapeDtypeStruct((1, NU), F32),
                ),
                in_specs=[vmem] * 2,
                out_specs=(vmem, vmem),
                compiler_params=pltpu.CompilerParams(vmem_limit_bytes=56 * 1024 * 1024),
                name="finish",
            )(primaries.reshape(wrows, outs, recv), filters)
        )

    placed = (
        P(None, "freq", None, "src"),
        P(None, "freq", None, "src"),
        P(None, "src"),
        P(),
        P(None, "freq", "src", None),
        P("freq"),
        P("freq"),
        P("freq", "src", None),
    )
    return jax.shard_map(
        body,
        mesh=mesh,
        in_specs=placed,
        out_specs=(P("freq", "src", None), P("freq", None)),
        check_vma=False,
    )
```
